256 devices in a mesh: stream: 64 (over z_hi, y, x), girth: 4 (over z_lo, core).
Axes of the slice: x: 4, y: 4, z: 8 (z_hi: 4, z_lo: 2; z = z_hi * 2 + z_lo), core: 2. Of those that a mesh axis runs over, the one named last changes fastest.
Arguments:
- eta_hat: float32 [4096, 4096], P('stream', 'girth'), may hold values from -0.0014648438 to 0.0014648438
- phi_hat: float32 [4096, 4096], P('stream', 'girth'), may hold values from -0.0014648438 to 0.0014648438
- zone_rows: int32 [64, 8], replicated, may hold values from 0 to 4095
- zone_count: int32 [64], P('stream'), may hold values from 1 to 8, as said below
- volume: float32 [512, 48, 4096], P('stream', None, 'girth'), may hold values from 0 to 1
- lift: float32 [512, 48, 4096], P('stream', None, 'girth'), may hold values from -3 to 3
- stream_speed: float32 [512, 48, 4096], P('stream', None, 'girth'), may hold values from 0.5 to 1.5
- surface_blocks: int32 [512, 6], P('stream'), may hold values 0 or 1
Outputs:
- volume_next: float32 [512, 48, 4096], P('stream', None, 'girth')
- lift_next: float32 [512, 48, 4096], P('stream', None, 'girth')
The draws below stay inside these ranges and needn't reach their ends.
Inputs may be any that keep to these rules, and one draw needn't show every extreme that they name: `zone_count`: each slab has 1 to 8 zone planes and some slab has exactly 8.
All inputs are finite; a program needn't handle non-finite values. No bound on the sum of `surface_blocks` on one device may be relied on, other than what follows from the above.
Results may differ from the reference program's by a relative error of at most 0.00017.
Values sent between devices are 32-bit elements; how exact they have to be, the bound alone decides.
A program may use at most 128 MiB of HBM per device.

```python
import math
import jax
import jax.numpy as jnp
from jax import lax

NX = 4096
NY = 4096
CXR = 8
NZ = 48
ZONE = 8
NXR = 512
N_STREAM = 64


def draw_zone_count(key, part):
    key = jax.random.fold_in(key, 7)
    key_counts, key_top = jax.random.split(key)
    counts = jax.random.randint(key_counts, (N_STREAM,), 1, ZONE + 1)
    top_slab = jax.random.randint(key_top, (), 0, N_STREAM)
    return jnp.where(jnp.arange(N_STREAM) == top_slab, ZONE, counts).astype(jnp.int32)


def plant(array, own_key, least, top_value):
    shape = array.shape
    index_at = [jax.random.randint(jax.random.fold_in(own_key, axis), (), 0, shape[axis]) for axis in range(len(shape))]
    array = array.at[tuple(index_at)].set(least)
    longest = shape.index(max(shape))
    index_at[longest] = (index_at[longest] + 1) % shape[longest]
    return array.at[tuple(index_at)].set(top_value)


def shard_levels(rng, shape, shards, smallest, high):
    loudness = 1.0
    for dim, blocks in shards:
        draws = jax.random.uniform(jax.random.fold_in(jax.random.fold_in(rng, 6), dim), (blocks,), jnp.float32, smallest / len(shards), high / len(shards))
        loudness = loudness * jnp.repeat(jnp.exp(draws), shape[dim] // blocks).reshape((-1,) + (1,) * (len(shape) - 1 - dim))
    return loudness


def scatter_about(own_key, dims, scale, limit, shards=(), kind=jnp.bfloat16):
    loudness = shard_levels(own_key, dims, shards, -0.22, 0.18) if shards else 1.0
    drawn = jax.random.normal(own_key, dims, jnp.float32) * scale * loudness
    return jnp.minimum(jnp.maximum(drawn, -limit), limit).astype(kind)


def setup_inputs(seed: int = 0) -> dict:
    streams_of = jax.random.split(jax.random.key(seed), 9)
    return {
        "eta_hat": scatter_about(streams_of[0], (NX, NY), (NX * NY) ** -0.5, 0.0014648438, ((0, 64), (1, 4)), jnp.float32),
        "phi_hat": scatter_about(streams_of[1], (NX, NY), (NX * NY) ** -0.5, 0.0014648438, ((0, 64), (1, 4)), jnp.float32),
        "zone_rows": plant(jax.random.randint(streams_of[2], (N_STREAM, ZONE), 0, NX), jax.random.fold_in(streams_of[2], 1), 0, NX - 1).astype(jnp.int32),
        "zone_count": draw_zone_count(jax.random.fold_in(streams_of[8], 71), 0),
        "volume": jnp.clip(1.0 * jax.random.uniform(streams_of[4], (NXR, NZ, NY), jnp.float32) ** shard_levels(streams_of[4], (NXR, NZ, NY), ((0, 64), (2, 4)), -0.2, 0.2), 0.0, 1.0),
        "lift": scatter_about(streams_of[5], (NXR, NZ, NY), 0.5, 3.0, ((0, 64), (2, 4)), jnp.float32),
        "stream_speed": jnp.clip(0.5 + 1.0 * jax.random.uniform(streams_of[6], (NXR, NZ, NY), jnp.float32) ** shard_levels(streams_of[6], (NXR, NZ, NY), ((0, 64), (2, 4)), -0.2, 0.2), 0.5, 1.5),
        "surface_blocks": plant((jax.random.randint(streams_of[7], (NXR, NZ // 8), 0, 2) < 1).astype(jnp.int32), jax.random.fold_in(streams_of[7], 1), 0, 1),
    }


depth_scale = 2.0
cell_height = 0.125

def signed_freq(mode_idx, extent):
    half_size = extent // 2
    shifted = jnp.where(mode_idx < half_size, mode_idx, mode_idx - extent)
    return 2.0 * shifted.astype(jnp.float32) / extent

def cas_pair(left_ids, right_ids, extent):
    phases = (left_ids[:, None] * right_ids[None, :] % extent).astype(jnp.float32) * (2.0 * math.pi / extent)
    return (jnp.cos(phases) + jnp.sin(phases), jnp.cos(phases) - jnp.sin(phases))

def hos_zone(eta_hat, phi_hat, zone_rows):
    highest = lax.Precision.HIGHEST
    kx_ids = jnp.arange(NX, dtype=jnp.int32)
    ky_ids = jnp.arange(NY, dtype=jnp.int32)
    freq_x = signed_freq(kx_ids, NX)
    freq_y = signed_freq(ky_ids, NY)
    wavenum = jnp.sqrt(freq_x[:, None] ** 2 + freq_y[None, :] ** 2)
    lift_hat = wavenum * jnp.tanh(depth_scale * wavenum) * phi_hat
    even_tab, odd_tab = cas_pair(ky_ids, ky_ids, NY)
    slope_tab = freq_y[:, None] * odd_tab
    y_done = jnp.dot(eta_hat, even_tab, precision=highest)
    y_slope = jnp.dot(eta_hat, slope_tab, precision=highest)
    y_lift = jnp.dot(lift_hat, even_tab, precision=highest)
    zone_list = zone_rows.reshape(-1)
    even_x, odd_x = cas_pair(zone_list, kx_ids, NX)
    slope_x = odd_x * freq_x[None, :]
    height = jnp.dot(even_x, y_done, precision=highest)
    tilt_x = jnp.dot(slope_x, y_done, precision=highest)
    tilt_y = jnp.dot(even_x, y_slope, precision=highest)
    surf_lift = jnp.dot(even_x, y_lift, precision=highest)
    rise_rate = (1.0 + tilt_x * tilt_x + tilt_y * tilt_y) * surf_lift
    return (height.reshape(N_STREAM, ZONE, NY), rise_rate.reshape(N_STREAM, ZONE, NY))

def relax(fraction, lift_now, height, rise_rate, zone_count):
    zone_span = fraction.shape[1]
    layers = fraction.shape[2]
    levels = (jnp.arange(layers, dtype=jnp.float32) - layers / 2 + 0.5) * cell_height
    gap_up = levels[None, None, :, None] - height[:, :, None, :]
    fraction_goal = jnp.clip(0.5 - gap_up / cell_height, 0.0, 1.0)
    lift_goal = rise_rate[:, :, None, :] * jnp.exp(0.5 * jnp.minimum(gap_up, 0.0))
    plane_idx = jnp.arange(zone_span, dtype=jnp.float32)[None, :]
    totals = zone_count.astype(jnp.float32)[:, None]
    stretch = jnp.minimum((plane_idx + 0.5) / totals, 1.0)
    weights = jnp.where(plane_idx < totals, 1.0 - (jnp.exp(stretch ** 3.5) - 1.0) / (math.e - 1.0), 0.0)
    weights = weights[:, :, None, None]
    return (weights * fraction_goal + (1.0 - weights) * fraction, weights * lift_goal + (1.0 - weights) * lift_now)

def advance(padded, surface_marks):
    flux_x = padded[0]
    volume_pad = padded[1]
    lift_pad = padded[2]
    fraction = volume_pad[1:-1, :, 1:-1]
    lift_now = lift_pad[1:-1, :, 1:-1]
    upwind = flux_x[1:-1, :, 1:-1] - flux_x[:-2, :, 1:-1]
    spread = volume_pad[1:-1, :, 2:] + volume_pad[1:-1, :, :-2] - 2.0 * fraction
    vertical = jnp.maximum(lift_now[:, :-1], 0.0) * fraction[:, :-1] + jnp.minimum(lift_now[:, :-1], 0.0) * fraction[:, 1:]
    boundary = jnp.zeros_like(fraction[:, :1])
    face_flux = jnp.concatenate([boundary, vertical, boundary], axis=1)
    divergence = face_flux[:, 1:] - face_flux[:, :-1]
    sharpen = surface_marks * fraction * (1.0 - fraction) * (2.0 * fraction - 1.0)
    volume_next = fraction - 0.3 * upwind - 0.3 * divergence + 0.1 * spread + 2.0 * sharpen
    padded_z = jnp.pad(lift_now, ((0, 0), (1, 1), (0, 0)))
    beside_all = lift_pad[2:, :, 1:-1] + lift_pad[:-2, :, 1:-1] + lift_pad[1:-1, :, 2:] + lift_pad[1:-1, :, :-2]
    beside_all = beside_all + padded_z[:, 2:] + padded_z[:, :-2]
    lift_next = lift_now + 0.15 * (beside_all - 6.0 * lift_now)
    return (volume_next, lift_next)

def reference(eta_hat, phi_hat, zone_rows, zone_count, volume, lift, stream_speed, surface_blocks):
    height, rise_rate = hos_zone(eta_hat, phi_hat, zone_rows)
    volume_slabs = volume.reshape(N_STREAM, CXR, NZ, NY)
    lift_slabs = lift.reshape(N_STREAM, CXR, NZ, NY)
    head_volume, head_lift = relax(volume_slabs[:, :ZONE], lift_slabs[:, :ZONE], height, rise_rate, zone_count)
    relaxed_volume = jnp.concatenate([head_volume, volume_slabs[:, ZONE:]], axis=1).reshape(NXR, NZ, NY)
    relaxed_lift = jnp.concatenate([head_lift, lift_slabs[:, ZONE:]], axis=1).reshape(NXR, NZ, NY)
    stacked = jnp.stack([stream_speed * relaxed_volume, relaxed_volume, relaxed_lift])
    padded = jnp.pad(stacked, ((0, 0), (1, 1), (0, 0), (1, 1)))
    surface_marks = jnp.repeat(surface_blocks, 8, axis=1)[:, :, None].astype(jnp.float32)
    return advance(padded, surface_marks)
```

```python
import math

import jax
import jax.numpy as jnp
from jax import lax
from jax.experimental import pallas as pl
from jax.experimental.pallas import tpu as pltpu
from jax.sharding import PartitionSpec as P

F32 = jnp.float32
BF16 = jnp.bfloat16
MESH = pl.DeviceIdType.MESH
EXT = 1280

AG, RS, RZ, GA, HP, HN, RAW = 0, 12, 24, 30, 33, 37, 41
N_SEM = 49


def iota(shape, dim):
    return lax.broadcasted_iota(jnp.int32, shape, dim)


def quarter_turns(t):
    k = jnp.floor(t + 0.5)
    r = t - k
    r2 = r * r
    s = r * (
        1.5707963267949
        + r2 * (-0.645964097506 + r2 * (0.0796926262462 + r2 * (-0.00468175413532 + r2 * 0.000160441184787)))
    )
    c = 1.0 + r2 * (
        -1.23370055013617
        + r2 * (0.253669507901 + r2 * (-0.0208634807634 + r2 * (0.000919260274839 - r2 * 2.52020423731e-5)))
    )
    half = jnp.floor(k * 0.5)
    odd = (k - 2.0 * half) > 0.5
    sign = 1.0 - 2.0 * (half - 2.0 * jnp.floor(half * 0.5))
    return sign, odd, c, s


def cas_dcas(t):
    sign, odd, c, s = quarter_turns(t)
    plus, minus = c + s, c - s
    return sign * jnp.where(odd, minus, plus), sign * jnp.where(odd, -plus, minus)


def cos_sin(t):
    sign, odd, c, s = quarter_turns(t)
    return sign * jnp.where(odd, -s, c), sign * jnp.where(odd, c, s)


def split(value):
    hi = value.astype(BF16)
    return hi, (value - hi.astype(F32)).astype(BF16)


def dot(left, right):
    return jnp.dot(left, right, preferred_element_type=F32)


def dot3(left, right):
    (lh, ll), (rh, rl) = left, right
    return dot(lh, rh) + (dot(lh, rl) + dot(ll, rh))


def pick(index, values):
    out = values[-1]
    for i in range(len(values) - 2, -1, -1):
        out = jnp.where(index == i, values[i], out)
    return out


def wave_kernel(
    zr_ref, zc_ref, eta, phi, vol, lft, spd,
    hr, planes, cols,
    ag, tab, ps, ob, nb, zs, zo, zn, xg, xp, hmsg, hp, hn, e_hi, e_lo, perm, lhs, uu, hh,
    ssem, rsem,
):
    s = lax.axis_index("stream")
    g = lax.axis_index("girth")
    zh, y, x = s // 16, (s // 4) % 4, s % 4

    def at(zh_, y_, x_):
        return (zh_ * 16 + y_ * 4 + x_, g)

    def turn(c, d):
        return lax.rem(c + d + 4, 4)

    def on_x(d):
        return at(zh, y, turn(x, d))

    def on_y(d):
        return at(zh, turn(y, d), x)

    def on_z(d):
        return at(turn(zh, d), y, x)

    s_next = lax.rem(s + 1, 64)
    s_prev = lax.rem(s + 63, 64)

    def girth(j):
        return lax.rem(g + j, 4)

    targets = [on_x(1), on_x(-1), on_y(1), on_y(-1), on_z(1), on_z(-1)]
    targets += [(s, girth(j)) for j in (1, 2, 3)]
    targets += [(s_next, girth(j)) for j in range(4)]
    targets += [(s_prev, girth(j)) for j in range(4)]
    barrier = pltpu.get_barrier_semaphore()
    for device in targets:
        pl.semaphore_signal(barrier, inc=1, device_id=device, device_id_type=MESH)
    pl.semaphore_wait(barrier, len(targets))

    def copy(src, dst, index, device):
        return pltpu.make_async_remote_copy(
            src_ref=src, dst_ref=dst, send_sem=ssem.at[index], recv_sem=rsem.at[index],
            device_id=device, device_id_type=MESH,
        )

    sent = []

    def start(src, dst, index, device):
        c = copy(src, dst, index, device)
        c.start()
        sent.append(c)
        return c

    first = (on_x, on_y)
    second = (on_y, on_x)

    gat = {}
    for q in range(2):
        cs = pl.ds(q * 512, 512)
        ag[q, 0, 0] = eta[:, cs]
        gat[q, 0] = start(ag.at[q, 0, 0], ag.at[q, 0, 1], AG + 6 * q, first[q](1))
        gat[q, 1] = start(ag.at[q, 0, 0], ag.at[q, 0, 2], AG + 6 * q + 1, first[q](-1))
    kx_own = (s * 64 + iota((64, 1), 0)).astype(F32)
    fx_own = kx_own / 2048.0 - jnp.where(kx_own >= 2048.0, 2.0, 0.0)
    for q in range(2):
        cs = pl.ds(q * 512, 512)
        ky = (g * 1024 + q * 512 + iota((1, 512), 1)).astype(F32)
        fy = ky / 2048.0 - jnp.where(ky >= 2048.0, 2.0, 0.0)
        rad = jnp.sqrt(fx_own * fx_own + fy * fy)
        ag[q, 1, 0] = rad * jnp.tanh(2.0 * rad) * phi[:, cs]
        gat[q, 2] = start(ag.at[q, 1, 0], ag.at[q, 1, 1], AG + 6 * q + 2, first[q](1))
        gat[q, 3] = start(ag.at[q, 1, 0], ag.at[q, 1, 2], AG + 6 * q + 3, first[q](-1))

    raw = []
    edge_left, edge_right = pl.ds(0, 128), pl.ds(896, 128)
    to_right, to_left = (s, girth(1)), (s, girth(3))
    raw.append(start(vol.at[:, :, edge_right], cols.at[0], RAW, to_right))
    raw.append(start(lft.at[:, :, edge_right], cols.at[1], RAW + 1, to_right))
    raw.append(start(vol.at[:, :, edge_left], cols.at[2], RAW + 2, to_left))
    raw.append(start(lft.at[:, :, edge_left], cols.at[3], RAW + 3, to_left))

    zr = zr_ref[...].astype(F32)
    lane64 = iota((8, 64), 1)
    lane256 = iota((1, 256), 1)
    slot = lane256 // 64
    rel = (0, 1, -1, 2)
    for q in range(2):
        here = x if q == 0 else y
        coords = [turn(here, d) for d in (0, -1, 1, 2)]
        if q == 0:
            slabs = [zh * 16 + y * 4 + c for c in coords]
        else:
            slabs = [zh * 16 + c * 4 + x for c in coords]
        kx = (pick(slot, slabs) * 64 + lane256 % 64).astype(F32)
        fx = kx / 2048.0 - jnp.where(kx >= 2048.0, 2.0, 0.0)
        for r in range(4):
            for z in range(4):
                zz = turn(zh, rel[z])
                want = zz * 16 + (turn(y, rel[r]) * 4 + x if q == 0 else y * 4 + turn(x, rel[r]))
                rows = jnp.sum(jnp.where(lane64 == want, zr, 0.0), axis=1, keepdims=True)
                t = rows * kx * (1.0 / 1024.0)
                even, odd = cas_dcas(t)
                tab[q, r, z, 0] = even
                tab[q, r, z, 1] = odd * fx

    for q in range(2):
        gat[q, 0].wait_recv()
        gat[q, 4] = start(ag.at[q, 0, 1], ag.at[q, 0, 3], AG + 6 * q + 4, first[q](1))
    for q in range(2):
        gat[q, 3].wait_recv()
        gat[q, 5] = start(ag.at[q, 1, 2], ag.at[q, 1, 3], AG + 6 * q + 5, first[q](-1))

    def fill_e(i, _):
        row = pl.multiple_of(i * 32, 32)
        a = (row + iota((32, 1), 0)).astype(F32)
        c = iota((1, 512), 1).astype(F32)
        co, si = cos_sin(a * c * (1.0 / 128.0))
        for k, value in enumerate((co, si)):
            hi, lo = split(value)
            e_hi[pl.ds(row, 32), k * 512 : (k + 1) * 512] = hi
            e_lo[pl.ds(row, 32), k * 512 : (k + 1) * 512] = lo
        return 0

    lax.fori_loop(0, 16, fill_e, 0)

    def fill_p(i, _):
        row = pl.multiple_of(i * 32, 32)
        a = row + iota((32, 1024), 0)
        b = iota((32, 1024), 1)
        perm[pl.ds(row, 32), :] = jnp.where(a == 8 * (b % 128) + b // 128, 1.0, 0.0).astype(BF16)
        return 0

    lax.fori_loop(0, 32, fill_p, 0)

    near, mid = {}, {}
    for q in range(2):
        for k in (1, 2, 4, 5):
            gat[q, k].wait_recv()
        table = tab[q]
        both = split(table.reshape(256, 256))
        even = split(table[:, :, 0].reshape(128, 256))
        acc = dot3(both, split(ag[q, 0].reshape(256, 512)))
        ps[q, :, :, 0:2] = acc.reshape(4, 4, 2, 8, 512)
        acc = dot3(even, split(ag[q, 1].reshape(256, 512)))
        ps[q, :, :, 2] = acc.reshape(4, 4, 8, 512)
        b = RS + 6 * q
        right, left = second[q](1), second[q](-1)
        near[q, 0] = start(ps.at[q, 3, pl.ds(0, 2)], ob.at[q, 0], b, right)
        near[q, 1] = start(ps.at[q, 3, pl.ds(2, 2)], ob.at[q, 1], b + 1, left)
        near[q, 2] = start(ps.at[q, 1, pl.ds(2, 2)], nb.at[q, 0, pl.ds(2, 2)], b + 2, right)
        near[q, 3] = start(ps.at[q, 2, pl.ds(0, 2)], nb.at[q, 1, pl.ds(0, 2)], b + 3, left)
    for q in range(2):
        b = RS + 6 * q
        right, left = second[q](1), second[q](-1)
        near[q, 0].wait_recv()
        ps[q, 1, 0:2] = ps[q, 1, 0:2] + ob[q, 0]
        near[q, 4] = start(ps.at[q, 1, pl.ds(0, 2)], nb.at[q, 0, pl.ds(0, 2)], b + 4, right)
        near[q, 1].wait_recv()
        ps[q, 2, 2:4] = ps[q, 2, 2:4] + ob[q, 1]
        near[q, 5] = start(ps.at[q, 2, pl.ds(2, 2)], nb.at[q, 1, pl.ds(2, 2)], b + 5, left)

    to_next, to_prev = (s_next, g), (s_prev, g)
    raw.append(start(vol.at[7], planes.at[0], RAW + 4, to_next))
    raw.append(start(spd.at[7], planes.at[1], RAW + 5, to_next))
    raw.append(start(lft.at[7], planes.at[2], RAW + 6, to_next))
    raw.append(start(lft.at[0], planes.at[3], RAW + 7, to_prev))

    right, left = on_z(1), on_z(-1)
    for q in range(2):
        for k in (2, 3, 4, 5):
            near[q, k].wait_recv()
        zs[q] = ps[q, 0] + nb[q, 0] + nb[q, 1]
        b = RZ + 3 * q
        ahead, back = (right, left) if q == 0 else (left, right)
        fore, aft = (1, 2) if q == 0 else (2, 1)
        mid[q, 0] = start(zs.at[q, 3], zo.at[q], b, ahead)
        mid[q, 1] = start(zs.at[q, aft], zn.at[q, 1], b + 1, back)
    for q in range(2):
        b = RZ + 3 * q
        ahead = right if q == 0 else left
        fore = 1 if q == 0 else 2
        mid[q, 0].wait_recv()
        zs[q, fore] = zs[q, fore] + zo[q]
        mid[q, 2] = start(zs.at[q, fore], zn.at[q, 0], b + 2, ahead)
    for q in range(2):
        mid[q, 1].wait_recv()
        mid[q, 2].wait_recv()
        xp[:, :, q * 512 : (q + 1) * 512] = zs[q, 0] + zn[q, 0] + zn[q, 1]

    hi, lo = split(xp[...].reshape(24, 1024))
    moved = dot(hi, perm[...]) + dot(lo, perm[...])
    moved = moved.reshape(3, 8, 1024)
    xg[g] = moved
    sub = iota((8, 1024), 0)
    count = jnp.full((8, 1024), zc_ref[0].astype(F32))
    head = jnp.where(sub == 6, count, 0.0)
    tail = jnp.where(sub == 7, count, 0.0)
    for k in range(3):
        head = jnp.where(sub == k, moved[k, 7:8], head)
        tail = jnp.where(sub == 3 + k, moved[k, 0:1], tail)
    hmsg[0] = head
    hmsg[1] = tail
    last = []
    for j in (1, 2, 3):
        last.append(start(xg.at[g], xg.at[g], GA + j - 1, (s, girth(j))))
    for j in range(4):
        last.append(start(hmsg.at[0], hp.at[g], HP + j, (s_next, girth(j))))
        last.append(start(hmsg.at[1], hn.at[g], HN + j, (s_prev, girth(j))))
    for c in last:
        c.wait_recv()

    for gg in range(4):
        halo = hp[gg] + hn[gg]
        for b in range(8):
            ks = slice(128 * b, 128 * (b + 1))
            os = slice(128 * gg, 128 * (gg + 1))
            ky = (1024 * gg + b + 8 * iota((1, 128), 1)).astype(F32)
            fy = ky * (1.0 / 2048.0) - (2.0 if gg >= 2 else 0.0)
            top = xg[gg, 0, :, ks]
            edge = halo[:, ks]
            lhs[b, 0:8, os] = top
            lhs[b, 8:16, os] = xg[gg, 1, :, ks]
            lhs[b, 16:24, os] = xg[gg, 2, :, ks]
            lhs[b, 24:32, os] = edge
            lhs[b, 32:40, os] = top * fy
            lhs[b, 40:48, os] = edge * fy
    uu[...] = dot3(split(lhs[...].reshape(384, 512)), (e_hi[...], e_lo[...])).reshape(8, 48, 1024)

    q8 = iota((16, 128), 0).astype(F32)
    places = [(2 * g - 1, 384)] + [(2 * g + i // 4, 128 * (i % 4)) for i in range(8)] + [(2 * g + 2, 0)]
    b8 = iota((8, 128), 0)
    for i, (block, c0) in enumerate(places):
        c = c0 + iota((8, 128), 1)
        t = (b8 * c).astype(F32) * (1.0 / 1024.0) + (b8 * block).astype(F32) * 0.5
        even, odd = cas_dcas(t)
        out = [jnp.zeros((8, 128), F32) for _ in range(6)]
        for b in range(8):
            ev, od = even[b : b + 1], odd[b : b + 1]
            for k in range(6):
                re = uu[b, 8 * k : 8 * k + 8, c0 : c0 + 128]
                im = uu[b, 8 * k : 8 * k + 8, 512 + c0 : 512 + c0 + 128]
                out[k] = out[k] + (re * ev + im * od if k < 4 else re * od - im * ev)
        cs = slice(128 * i, 128 * (i + 1))
        for k in range(6):
            hh[k, :, cs] = out[k]

    def weights(plane, count):
        q_ = jnp.minimum((plane + 0.5) / count, 1.0)
        w_ = 1.0 - (jnp.exp(q_ * q_ * q_ * jnp.sqrt(q_)) - 1.0) / (math.e - 1.0)
        return jnp.where(plane < count, w_, 0.0)

    def put(planes_, cs, height, tilt_x, lift, tilt_y, w):
        rise = (1.0 + tilt_x * tilt_x + tilt_y * tilt_y) * lift
        parts = (0.5 + 8.0 * height, jnp.exp(-0.5 * height), w * rise, w)
        for i, plane in enumerate(planes_):
            for k in range(4):
                hr[plane, k : k + 1, cs] = parts[k][i : i + 1]

    own_w = weights(iota((8, 128), 0).astype(F32), jnp.full((8, 128), zc_ref[0].astype(F32)))
    prev_w = weights(jnp.full((1, 128), 7.0, F32), hp[0, 6:7, 0:128])
    next_w = weights(jnp.full((1, 128), 0.0, F32), hn[0, 7:8, 0:128])
    for i in range(10):
        cs = slice(128 * i, 128 * (i + 1))
        put(range(8), cs, hh[0, :, cs], hh[1, :, cs], hh[2, :, cs], hh[4, :, cs], own_w)
        put((8,), cs, hh[3, 0:1, cs], hh[3, 1:2, cs], hh[3, 2:3, cs], hh[5, 0:1, cs], prev_w)
        put((9,), cs, hh[3, 3:4, cs], hh[3, 4:5, cs], hh[3, 5:6, cs], hh[5, 3:4, cs], next_w)

    for c in raw:
        c.wait_recv()
    for c in sent:
        c.wait_send()


def wave_part(zr, zone_count, eta, phi, vol, lft, spd):
    vmem = pl.BlockSpec(memory_space=pltpu.VMEM)
    anyw = pl.BlockSpec(memory_space=pl.ANY)
    return pl.pallas_call(
        wave_kernel,
        out_shape=(
            jax.ShapeDtypeStruct((10, 4, EXT), F32),
            jax.ShapeDtypeStruct((4, 48, 1024), F32),
            jax.ShapeDtypeStruct((4, 8, 48, 128), F32),
        ),
        in_specs=[vmem, pl.BlockSpec(memory_space=pltpu.SMEM), vmem, vmem, anyw, anyw, anyw],
        out_specs=(vmem, anyw, anyw),
        scratch_shapes=[
            pltpu.VMEM((2, 2, 4, 64, 512), F32),
            pltpu.VMEM((2, 4, 4, 2, 8, 256), F32),
            pltpu.VMEM((2, 4, 4, 3, 8, 512), F32),
            pltpu.VMEM((2, 2, 2, 3, 8, 512), F32),
            pltpu.VMEM((2, 2, 4, 3, 8, 512), F32),
            pltpu.VMEM((2, 4, 3, 8, 512), F32),
            pltpu.VMEM((2, 3, 8, 512), F32),
            pltpu.VMEM((2, 2, 3, 8, 512), F32),
            pltpu.VMEM((4, 3, 8, 1024), F32),
            pltpu.VMEM((3, 8, 1024), F32),
            pltpu.VMEM((2, 8, 1024), F32),
            pltpu.VMEM((4, 8, 1024), F32),
            pltpu.VMEM((4, 8, 1024), F32),
            pltpu.VMEM((512, 1024), BF16),
            pltpu.VMEM((512, 1024), BF16),
            pltpu.VMEM((1024, 1024), BF16),
            pltpu.VMEM((8, 48, 512), F32),
            pltpu.VMEM((8, 48, 1024), F32),
            pltpu.VMEM((6, 8, EXT), F32),
            pltpu.SemaphoreType.DMA((N_SEM,)),
            pltpu.SemaphoreType.DMA((N_SEM,)),
        ],
        compiler_params=pltpu.CompilerParams(
            collective_id=0, has_side_effects=True, vmem_limit_bytes=40 * 1024 * 1024
        ),
        name="wave_part",
    )(zr, zone_count, eta, phi, vol, lft, spd)


def field_kernel(marks, hr, planes, cols, vol, lft, spd, vol_out, lft_out, rv, rl, fx):
    t = pl.program_id(0)
    s = lax.axis_index("stream")
    g = lax.axis_index("girth")
    level8 = iota((48, 128), 0).astype(F32) - 23.5
    rise_z = jnp.exp(level8 * 0.0625)
    lane = iota((48, 128), 1)
    row = iota((48, 128), 0)

    def surface(plane, i):
        cs = slice(128 * i, 128 * (i + 1))
        return [hr[plane, k : k + 1, cs] for k in range(4)]

    def relax_v(v, here):
        goal = jnp.clip(here[0] - level8, 0.0, 1.0)
        return here[3] * goal + (1.0 - here[3]) * v

    def relax_l(l, here):
        return here[2] * jnp.minimum(rise_z * here[1], 1.0) + (1.0 - here[3]) * l

    def group(i):
        return slice(128 * i, 128 * (i + 1))

    now = lax.rem(t, 3)
    one = lax.rem(t + 2, 3)
    two = lax.rem(t + 1, 3)

    @pl.when(t < 8)
    def _():
        for i in range(8):
            here = surface(t, i + 1)
            v = relax_v(vol[0, :, group(i)], here)
            rv[now, :, group(i)] = v
            fx[now, :, group(i)] = spd[0, :, group(i)] * v
            rl[now, :, group(i)] = relax_l(lft[0, :, group(i)], here)

    @pl.when(t == 0)
    def _():
        for i in range(8):
            here = surface(8, i + 1)
            v = relax_v(planes[0, :, group(i)], here)
            l = relax_l(planes[2, :, group(i)], here)
            fx[2, :, group(i)] = jnp.where(s > 0, planes[1, :, group(i)] * v, 0.0)
            rl[2, :, group(i)] = jnp.where(s > 0, l, 0.0)

    @pl.when(t == 8)
    def _():
        for i in range(8):
            l = relax_l(planes[3, :, group(i)], surface(9, i + 1))
            rl[2, :, group(i)] = jnp.where(s < 63, l, 0.0)

    @pl.when(t >= 1)
    def _():
        u = t - 1
        mark2 = jnp.concatenate(
            [jnp.full((8, 128), 2.0 * marks[u, k].astype(F32), F32) for k in range(6)], axis=0
        )
        here = surface(u, 0)
        v_left = jnp.where(g > 0, relax_v(cols[0, u], here), 0.0)
        l_left = jnp.where(g > 0, relax_l(cols[1, u], here), 0.0)
        here = surface(u, 9)
        v_right = jnp.where(g < 3, relax_v(cols[2, u], here), 0.0)
        l_right = jnp.where(g < 3, relax_l(cols[3, u], here), 0.0)
        v = rv[one, :, group(0)]
        l = rl[one, :, group(0)]
        v_fore, l_fore = pltpu.roll(v_left, 1, 1), pltpu.roll(l_left, 1, 1)
        v_back, l_back = pltpu.roll(v, 127, 1), pltpu.roll(l, 127, 1)
        for i in range(8):
            if i < 7:
                v_then, l_then = rv[one, :, group(i + 1)], rl[one, :, group(i + 1)]
            else:
                v_then, l_then = v_right, l_right
            v_fore_own, l_fore_own = pltpu.roll(v, 1, 1), pltpu.roll(l, 1, 1)
            v_back_then, l_back_then = pltpu.roll(v_then, 127, 1), pltpu.roll(l_then, 127, 1)
            v_y = jnp.where(lane == 0, v_fore, v_fore_own) + jnp.where(lane == 127, v_back_then, v_back)
            l_y = jnp.where(lane == 0, l_fore, l_fore_own) + jnp.where(lane == 127, l_back_then, l_back)
            face = jnp.maximum(l, 0.0) * v + jnp.minimum(l, 0.0) * pltpu.roll(v, 47, 0)
            face = jnp.where(row == 47, 0.0, face)
            div = face - pltpu.roll(face, 1, 0)
            upwind = fx[one, :, group(i)] - fx[two, :, group(i)]
            sharpen = mark2 * (v * (1.0 - v) * (2.0 * v - 1.0))
            vol_out[0, :, group(i)] = v - 0.3 * (upwind + div) + 0.1 * (v_y - 2.0 * v) + sharpen
            l_z = jnp.where(row == 47, 0.0, pltpu.roll(l, 47, 0)) + jnp.where(row == 0, 0.0, pltpu.roll(l, 1, 0))
            l_x = rl[now, :, group(i)] + rl[two, :, group(i)]
            lft_out[0, :, group(i)] = l + 0.15 * (l_x + l_y + l_z - 6.0 * l)
            v, l = v_then, l_then
            v_fore, l_fore, v_back, l_back = v_fore_own, l_fore_own, v_back_then, l_back_then


def field_part(marks, hr, planes, cols, vol, lft, spd):
    vmem = pl.BlockSpec(memory_space=pltpu.VMEM)
    plane = pl.BlockSpec((1, 48, 1024), lambda t: (jnp.minimum(t, 7), 0, 0))
    out = pl.BlockSpec((1, 48, 1024), lambda t: (jnp.maximum(t - 1, 0), 0, 0))
    return pl.pallas_call(
        field_kernel,
        grid=(9,),
        out_shape=(jax.ShapeDtypeStruct((8, 48, 1024), F32),) * 2,
        in_specs=[pl.BlockSpec(memory_space=pltpu.SMEM), vmem, vmem, vmem, plane, plane, plane],
        out_specs=(out, out),
        scratch_shapes=[pltpu.VMEM((3, 48, 1024), F32)] * 3,
        compiler_params=pltpu.CompilerParams(vmem_limit_bytes=32 * 1024 * 1024),
        name="field_part",
    )(marks, hr, planes, cols, vol, lft, spd)


def on_device(eta_hat, phi_hat, zone_rows, zone_count, volume, lift, stream_speed, surface_blocks):
    hr, planes, cols = wave_part(zone_rows.T, zone_count, eta_hat, phi_hat, volume, lift, stream_speed)
    return field_part(surface_blocks, hr, planes, cols, volume, lift, stream_speed)


def solution(mesh):
    return jax.shard_map(
        on_device,
        mesh=mesh,
        in_specs=(
            P("stream", "girth"),
            P("stream", "girth"),
            P(),
            P("stream"),
            P("stream", None, "girth"),
            P("stream", None, "girth"),
            P("stream", None, "girth"),
            P("stream", None),
        ),
        out_specs=(P("stream", None, "girth"), P("stream", None, "girth")),
        check_vma=False,
    )
```

```python
import math

import jax
import jax.numpy as jnp
from jax import lax
from jax.experimental import pallas as pl
from jax.experimental.pallas import tpu as pltpu
from jax.sharding import PartitionSpec as P

F32 = jnp.float32
BF16 = jnp.bfloat16
MESH = pl.DeviceIdType.MESH
EXT = 1280

AG, RS, RZ, GA, ROWS, COLS, PLANES, RELAY = 0, 12, 24, 30, 33, 35, 39, 43
N_SEM = 47


def iota(shape, dim):
    return lax.broadcasted_iota(jnp.int32, shape, dim)


def quarter_turns(t):
    k = jnp.floor(t + 0.5)
    r = t - k
    r2 = r * r
    s = r * (
        1.5707963267949
        + r2 * (-0.645964097506 + r2 * (0.0796926262462 + r2 * (-0.00468175413532 + r2 * 0.000160441184787)))
    )
    c = 1.0 + r2 * (
        -1.23370055013617
        + r2 * (0.253669507901 + r2 * (-0.0208634807634 + r2 * (0.000919260274839 - r2 * 2.52020423731e-5)))
    )
    half = jnp.floor(k * 0.5)
    odd = (k - 2.0 * half) > 0.5
    sign = 1.0 - 2.0 * (half - 2.0 * jnp.floor(half * 0.5))
    return sign, odd, c, s


def cas_dcas(t):
    sign, odd, c, s = quarter_turns(t)
    plus, minus = c + s, c - s
    return sign * jnp.where(odd, minus, plus), sign * jnp.where(odd, -plus, minus)


def cos_sin(t):
    sign, odd, c, s = quarter_turns(t)
    return sign * jnp.where(odd, -s, c), sign * jnp.where(odd, c, s)


def split(value):
    hi = value.astype(BF16)
    return hi, (value - hi.astype(F32)).astype(BF16)


def dot(left, right):
    return jnp.dot(left, right, preferred_element_type=F32)


def dot3(left, right):
    (lh, ll), (rh, rl) = left, right
    return dot(lh, rh) + (dot(lh, rl) + dot(ll, rh))


def pick(index, values):
    out = values[-1]
    for i in range(len(values) - 2, -1, -1):
        out = jnp.where(index == i, values[i], out)
    return out


def wave_kernel(
    zr_hbm, zc_ref, eta, phi_hbm, vol, lft, spd,
    hr, planes, cols,
    ag, tab, ps, ob, nb, zs, zo, zn, xg, xp, e_hi, e_lo, perm, lhs, uu, hh, relay, zr_ref, phi,
    ssem, rsem, lsem,
):
    s = lax.axis_index("stream")
    g = lax.axis_index("girth")
    zh, y, x = s // 16, (s // 4) % 4, s % 4

    def at(zh_, y_, x_):
        return (zh_ * 16 + y_ * 4 + x_, g)

    def turn(c, d):
        return lax.rem(c + d + 4, 4)

    def on_x(d):
        return at(zh, y, turn(x, d))

    def on_y(d):
        return at(zh, turn(y, d), x)

    def on_z(d):
        return at(turn(zh, d), y, x)

    fetched = [
        pltpu.make_async_copy(eta.at[:, pl.ds(0, 512)], ag.at[0, 0, 0], lsem.at[0]),
        pltpu.make_async_copy(eta.at[:, pl.ds(512, 512)], ag.at[1, 0, 0], lsem.at[1]),
        pltpu.make_async_copy(phi_hbm, phi, lsem.at[2]),
        pltpu.make_async_copy(zr_hbm, zr_ref, lsem.at[3]),
    ]
    for c in fetched:
        c.start()

    s_next = lax.rem(s + 1, 64)
    s_prev = lax.rem(s + 63, 64)

    def girth(j):
        return lax.rem(g + j, 4)

    targets = [on_x(1), on_x(-1), on_y(1), on_y(-1), on_z(1), on_z(-1)]
    targets += [(s, girth(j)) for j in (1, 2, 3)]
    targets += [(s_next, g), (s_prev, g), at(zh, 3 - y, 3 - x)]
    barrier = pltpu.get_barrier_semaphore()
    for device in targets:
        pl.semaphore_signal(barrier, inc=1, device_id=device, device_id_type=MESH)
    pl.semaphore_wait(barrier, len(targets))

    def copy(src, dst, index, device):
        return pltpu.make_async_remote_copy(
            src_ref=src, dst_ref=dst, send_sem=ssem.at[index], recv_sem=rsem.at[index],
            device_id=device, device_id_type=MESH,
        )

    sent = []

    def start(src, dst, index, device):
        c = copy(src, dst, index, device)
        c.start()
        sent.append(c)
        return c

    first = (on_x, on_y)
    second = (on_y, on_x)

    gat = {}
    for q in range(2):
        fetched[q].wait()
        gat[q, 0] = start(ag.at[q, 0, 0], ag.at[q, 0, 1], AG + 6 * q, first[q](1))
        gat[q, 1] = start(ag.at[q, 0, 0], ag.at[q, 0, 2], AG + 6 * q + 1, first[q](-1))
    high_edge = jnp.logical_and(x == 3, y == 3)
    low_edge = jnp.logical_and(x == 0, y == 0)

    up = [
        copy(f.at[7], relay.at[k], RELAY + k, on_z(1)) for k, f in enumerate((vol, spd, lft))
    ]
    down = copy(lft.at[0], relay.at[0], RELAY + 3, on_z(-1))

    @pl.when(high_edge)
    def _():
        for c in up:
            c.start()

    @pl.when(low_edge)
    def _():
        down.start()

    fetched[2].wait()
    kx_own = (s * 64 + iota((64, 1), 0)).astype(F32)
    fx_own = kx_own / 2048.0 - jnp.where(kx_own >= 2048.0, 2.0, 0.0)
    for q in range(2):
        cs = pl.ds(q * 512, 512)
        ky = (g * 1024 + q * 512 + iota((1, 512), 1)).astype(F32)
        fy = ky / 2048.0 - jnp.where(ky >= 2048.0, 2.0, 0.0)
        rad = jnp.sqrt(fx_own * fx_own + fy * fy)
        ag[q, 1, 0] = rad * jnp.tanh(2.0 * rad) * phi[:, cs]
        gat[q, 2] = start(ag.at[q, 1, 0], ag.at[q, 1, 1], AG + 6 * q + 2, first[q](1))
        gat[q, 3] = start(ag.at[q, 1, 0], ag.at[q, 1, 2], AG + 6 * q + 3, first[q](-1))

    raw = []
    edge_left, edge_right = pl.ds(0, 128), pl.ds(896, 128)
    to_right, to_left = (s, girth(1)), (s, girth(3))
    raw.append(start(vol.at[:, :, edge_right], cols.at[0], COLS, to_right))
    raw.append(start(lft.at[:, :, edge_right], cols.at[1], COLS + 1, to_right))
    raw.append(start(vol.at[:, :, edge_left], cols.at[2], COLS + 2, to_left))
    raw.append(start(lft.at[:, :, edge_left], cols.at[3], COLS + 3, to_left))

    fetched[3].wait()
    zr = zr_ref[...].astype(F32)
    lane64 = iota((8, 64), 1)
    lane256 = iota((1, 256), 1)
    slot = lane256 // 64
    rel = (0, 1, -1, 2)
    for q in range(2):
        here = x if q == 0 else y
        coords = [turn(here, d) for d in (0, -1, 1, 2)]
        if q == 0:
            slabs = [zh * 16 + y * 4 + c for c in coords]
        else:
            slabs = [zh * 16 + c * 4 + x for c in coords]
        kx = (pick(slot, slabs) * 64 + lane256 % 64).astype(F32)
        fx = kx / 2048.0 - jnp.where(kx >= 2048.0, 2.0, 0.0)
        for r in range(4):
            for z in range(4):
                zz = turn(zh, rel[z])
                want = zz * 16 + (turn(y, rel[r]) * 4 + x if q == 0 else y * 4 + turn(x, rel[r]))
                rows = jnp.sum(jnp.where(lane64 == want, zr, 0.0), axis=1, keepdims=True)
                t = rows * kx * (1.0 / 1024.0)
                even, odd = cas_dcas(t)
                tab[q, r, z, 0] = even
                tab[q, r, z, 1] = odd * fx

    for q in range(2):
        gat[q, 0].wait_recv()
        gat[q, 4] = start(ag.at[q, 0, 1], ag.at[q, 0, 3], AG + 6 * q + 4, first[q](1))
    for q in range(2):
        gat[q, 3].wait_recv()
        gat[q, 5] = start(ag.at[q, 1, 2], ag.at[q, 1, 3], AG + 6 * q + 5, first[q](-1))

    def fill_e(i, _):
        row = pl.multiple_of(i * 32, 32)
        a = (row + iota((32, 1), 0)).astype(F32)
        c = iota((1, 512), 1).astype(F32)
        co, si = cos_sin(a * c * (1.0 / 128.0))
        for k, value in enumerate((co, si)):
            hi, lo = split(value)
            e_hi[pl.ds(row, 32), k * 512 : (k + 1) * 512] = hi
            e_lo[pl.ds(row, 32), k * 512 : (k + 1) * 512] = lo
        return 0

    lax.fori_loop(0, 16, fill_e, 0)

    def fill_p(i, _):
        row = pl.multiple_of(i * 32, 32)
        a = row + iota((32, 1024), 0)
        b = iota((32, 1024), 1)
        perm[pl.ds(row, 32), :] = jnp.where(a == 8 * (b % 128) + b // 128, 1.0, 0.0).astype(BF16)
        return 0

    lax.fori_loop(0, 32, fill_p, 0)

    near, mid = {}, {}
    for q in range(2):
        for k in (1, 2, 4, 5):
            gat[q, k].wait_recv()
        table = tab[q]
        both = split(table.reshape(256, 256))
        even = split(table[:, :, 0].reshape(128, 256))
        acc = dot3(both, split(ag[q, 0].reshape(256, 512)))
        ps[q, :, :, 0:2] = acc.reshape(4, 4, 2, 8, 512)
        acc = dot3(even, split(ag[q, 1].reshape(256, 512)))
        ps[q, :, :, 2] = acc.reshape(4, 4, 8, 512)
        b = RS + 6 * q
        right, left = second[q](1), second[q](-1)
        near[q, 0] = start(ps.at[q, 3, pl.ds(0, 2)], ob.at[q, 0], b, right)
        near[q, 1] = start(ps.at[q, 3, pl.ds(2, 2)], ob.at[q, 1], b + 1, left)
        near[q, 2] = start(ps.at[q, 1, pl.ds(2, 2)], nb.at[q, 0, pl.ds(2, 2)], b + 2, right)
        near[q, 3] = start(ps.at[q, 2, pl.ds(0, 2)], nb.at[q, 1, pl.ds(0, 2)], b + 3, left)
    for q in range(2):
        b = RS + 6 * q
        right, left = second[q](1), second[q](-1)
        near[q, 0].wait_recv()
        ps[q, 1, 0:2] = ps[q, 1, 0:2] + ob[q, 0]
        near[q, 4] = start(ps.at[q, 1, pl.ds(0, 2)], nb.at[q, 0, pl.ds(0, 2)], b + 4, right)
        near[q, 1].wait_recv()
        ps[q, 2, 2:4] = ps[q, 2, 2:4] + ob[q, 1]
        near[q, 5] = start(ps.at[q, 2, pl.ds(2, 2)], nb.at[q, 1, pl.ds(2, 2)], b + 5, left)

    onward = [copy(f.at[7], planes.at[k], PLANES + k, (s_next, g)) for k, f in enumerate((vol, spd, lft))]
    onward_far = [copy(relay.at[k], planes.at[k], PLANES + k, at(zh, 0, 0)) for k in range(3)]
    backward = copy(lft.at[0], planes.at[3], PLANES + 3, (s_prev, g))
    backward_far = copy(relay.at[0], planes.at[3], PLANES + 3, at(zh, 3, 3))

    @pl.when(high_edge)
    def _():
        for k in range(3):
            up[k].wait_recv()
            onward_far[k].start()

    @pl.when(jnp.logical_not(high_edge))
    def _():
        for c in onward:
            c.start()

    @pl.when(low_edge)
    def _():
        down.wait_recv()
        backward_far.start()

    @pl.when(jnp.logical_not(low_edge))
    def _():
        backward.start()

    right, left = on_z(1), on_z(-1)
    for q in range(2):
        for k in (2, 3, 4, 5):
            near[q, k].wait_recv()
        zs[q] = ps[q, 0] + nb[q, 0] + nb[q, 1]
        b = RZ + 3 * q
        ahead, back = (right, left) if q == 0 else (left, right)
        fore, aft = (1, 2) if q == 0 else (2, 1)
        mid[q, 0] = start(zs.at[q, 3], zo.at[q], b, ahead)
        mid[q, 1] = start(zs.at[q, aft], zn.at[q, 1], b + 1, back)
    for q in range(2):
        b = RZ + 3 * q
        ahead = right if q == 0 else left
        fore = 1 if q == 0 else 2
        mid[q, 0].wait_recv()
        zs[q, fore] = zs[q, fore] + zo[q]
        mid[q, 2] = start(zs.at[q, fore], zn.at[q, 0], b + 2, ahead)
    for q in range(2):
        mid[q, 1].wait_recv()
        mid[q, 2].wait_recv()
        xp[:, :, q * 512 : (q + 1) * 512] = zs[q, 0] + zn[q, 0] + zn[q, 1]

    hi, lo = split(xp[...].reshape(24, 1024))
    moved = dot(hi, perm[...]) + dot(lo, perm[...])
    moved = moved.reshape(3, 8, 1024)
    xg[g] = moved
    last = []
    for j in (1, 2, 3):
        last.append(start(xg.at[g], xg.at[g], GA + j - 1, (s, girth(j))))
    for c in last:
        c.wait_recv()

    for gg in range(4):
        os = slice(128 * gg, 128 * (gg + 1))
        for b in range(8):
            ks = slice(128 * b, 128 * (b + 1))
            ky = (1024 * gg + b + 8 * iota((1, 128), 1)).astype(F32)
            fy = ky * (1.0 / 2048.0) - (2.0 if gg >= 2 else 0.0)
            top = xg[gg, 0, :, ks]
            lhs[b, 0:8, os] = top
            lhs[b, 8:16, os] = xg[gg, 1, :, ks]
            lhs[b, 16:24, os] = xg[gg, 2, :, ks]
            lhs[b, 24:32, os] = top * fy
    uu[...] = dot3(split(lhs[...].reshape(256, 512)), (e_hi[...], e_lo[...])).reshape(8, 32, 1024)

    places = [(2 * g - 1, 384)] + [(2 * g + i // 4, 128 * (i % 4)) for i in range(8)] + [(2 * g + 2, 0)]
    b8 = iota((8, 128), 0)
    for i, (block, c0) in enumerate(places):
        c = c0 + iota((8, 128), 1)
        t = (b8 * c).astype(F32) * (1.0 / 1024.0) + (b8 * block).astype(F32) * 0.5
        even, odd = cas_dcas(t)
        out = [jnp.zeros((8, 128), F32) for _ in range(4)]
        for b in range(8):
            ev, od = even[b : b + 1], odd[b : b + 1]
            for k in range(4):
                re = uu[b, 8 * k : 8 * k + 8, c0 : c0 + 128]
                im = uu[b, 8 * k : 8 * k + 8, 512 + c0 : 512 + c0 + 128]
                out[k] = out[k] + (re * ev + im * od if k < 3 else re * od - im * ev)
        cs = slice(128 * i, 128 * (i + 1))
        for k in range(4):
            hh[k, :, cs] = out[k]

    plane = iota((8, 128), 0).astype(F32)
    count = jnp.full((8, 128), zc_ref[0].astype(F32))
    q_ = jnp.minimum((plane + 0.5) / count, 1.0)
    w = 1.0 - (jnp.exp(q_ * q_ * q_ * jnp.sqrt(q_)) - 1.0) / (math.e - 1.0)
    w = jnp.where(plane < count, w, 0.0)
    for i in range(10):
        cs = slice(128 * i, 128 * (i + 1))
        height, tilt_x, lift, tilt_y = (hh[k, :, cs] for k in range(4))
        rise = (1.0 + tilt_x * tilt_x + tilt_y * tilt_y) * lift
        parts = (0.5 + 8.0 * height, jnp.exp(-0.5 * height), w * rise, w)
        for p in range(8):
            for k in range(4):
                hr[p, k : k + 1, cs] = parts[k][p : p + 1]

    rows = [
        start(hr.at[7], hr.at[8], ROWS, (s_next, g)),
        start(hr.at[0], hr.at[9], ROWS + 1, (s_prev, g)),
    ]

    for c in raw + rows + onward + [backward]:
        c.wait_recv()
    for c in sent:
        c.wait_send()

    @pl.when(high_edge)
    def _():
        for c in up + onward_far:
            c.wait_send()

    @pl.when(jnp.logical_not(high_edge))
    def _():
        for c in onward:
            c.wait_send()

    @pl.when(low_edge)
    def _():
        down.wait_send()
        backward_far.wait_send()

    @pl.when(jnp.logical_not(low_edge))
    def _():
        backward.wait_send()


def wave_part(zr, zone_count, eta, phi, vol, lft, spd):
    vmem = pl.BlockSpec(memory_space=pltpu.VMEM)
    anyw = pl.BlockSpec(memory_space=pl.ANY)
    return pl.pallas_call(
        wave_kernel,
        out_shape=(
            jax.ShapeDtypeStruct((10, 4, EXT), F32),
            jax.ShapeDtypeStruct((4, 48, 1024), F32),
            jax.ShapeDtypeStruct((4, 8, 48, 128), F32),
        ),
        in_specs=[anyw, pl.BlockSpec(memory_space=pltpu.SMEM), anyw, anyw, anyw, anyw, anyw],
        out_specs=(vmem, anyw, anyw),
        scratch_shapes=[
            pltpu.VMEM((2, 2, 4, 64, 512), F32),
            pltpu.VMEM((2, 4, 4, 2, 8, 256), F32),
            pltpu.VMEM((2, 4, 4, 3, 8, 512), F32),
            pltpu.VMEM((2, 2, 2, 3, 8, 512), F32),
            pltpu.VMEM((2, 2, 4, 3, 8, 512), F32),
            pltpu.VMEM((2, 4, 3, 8, 512), F32),
            pltpu.VMEM((2, 3, 8, 512), F32),
            pltpu.VMEM((2, 2, 3, 8, 512), F32),
            pltpu.VMEM((4, 3, 8, 1024), F32),
            pltpu.VMEM((3, 8, 1024), F32),
            pltpu.VMEM((512, 1024), BF16),
            pltpu.VMEM((512, 1024), BF16),
            pltpu.VMEM((1024, 1024), BF16),
            pltpu.VMEM((8, 32, 512), F32),
            pltpu.VMEM((8, 32, 1024), F32),
            pltpu.VMEM((4, 8, EXT), F32),
            pltpu.VMEM((3, 48, 1024), F32),
            pltpu.VMEM((8, 64), jnp.int32),
            pltpu.VMEM((64, 1024), F32),
            pltpu.SemaphoreType.DMA((N_SEM,)),
            pltpu.SemaphoreType.DMA((N_SEM,)),
            pltpu.SemaphoreType.DMA((4,)),
        ],
        compiler_params=pltpu.CompilerParams(
            collective_id=0, has_side_effects=True, vmem_limit_bytes=60 * 1024 * 1024
        ),
        name="wave_part",
    )(zr, zone_count, eta, phi, vol, lft, spd)


def field_kernel(marks, hr, planes, cols, vol, lft, spd, vol_out, lft_out, rv, rl, fx):
    t = pl.program_id(0)
    s = lax.axis_index("stream")
    g = lax.axis_index("girth")
    level8 = iota((48, 128), 0).astype(F32) - 23.5
    rise_z = jnp.exp(level8 * 0.0625)
    lane = iota((48, 128), 1)
    row = iota((48, 128), 0)

    def surface(plane, i):
        cs = slice(128 * i, 128 * (i + 1))
        return [hr[plane, k : k + 1, cs] for k in range(4)]

    def relax_v(v, here):
        goal = jnp.clip(here[0] - level8, 0.0, 1.0)
        return here[3] * goal + (1.0 - here[3]) * v

    def relax_l(l, here):
        return here[2] * jnp.minimum(rise_z * here[1], 1.0) + (1.0 - here[3]) * l

    def group(i):
        return slice(128 * i, 128 * (i + 1))

    now = lax.rem(t, 3)
    one = lax.rem(t + 2, 3)
    two = lax.rem(t + 1, 3)

    @pl.when(t < 8)
    def _():
        for i in range(8):
            here = surface(t, i + 1)
            v = relax_v(vol[0, :, group(i)], here)
            rv[now, :, group(i)] = v
            fx[now, :, group(i)] = spd[0, :, group(i)] * v
            rl[now, :, group(i)] = relax_l(lft[0, :, group(i)], here)

    @pl.when(t == 0)
    def _():
        for i in range(8):
            here = surface(8, i + 1)
            v = relax_v(planes[0, :, group(i)], here)
            l = relax_l(planes[2, :, group(i)], here)
            fx[2, :, group(i)] = jnp.where(s > 0, planes[1, :, group(i)] * v, 0.0)
            rl[2, :, group(i)] = jnp.where(s > 0, l, 0.0)

    @pl.when(t == 8)
    def _():
        for i in range(8):
            l = relax_l(planes[3, :, group(i)], surface(9, i + 1))
            rl[2, :, group(i)] = jnp.where(s < 63, l, 0.0)

    @pl.when(t >= 1)
    def _():
        u = t - 1
        mark2 = jnp.concatenate(
            [jnp.full((8, 128), 2.0 * marks[u, k].astype(F32), F32) for k in range(6)], axis=0
        )
        here = surface(u, 0)
        v_left = jnp.where(g > 0, relax_v(cols[0, u], here), 0.0)
        l_left = jnp.where(g > 0, relax_l(cols[1, u], here), 0.0)
        here = surface(u, 9)
        v_right = jnp.where(g < 3, relax_v(cols[2, u], here), 0.0)
        l_right = jnp.where(g < 3, relax_l(cols[3, u], here), 0.0)
        v = rv[one, :, group(0)]
        l = rl[one, :, group(0)]
        v_fore, l_fore = pltpu.roll(v_left, 1, 1), pltpu.roll(l_left, 1, 1)
        v_back, l_back = pltpu.roll(v, 127, 1), pltpu.roll(l, 127, 1)
        for i in range(8):
            if i < 7:
                v_then, l_then = rv[one, :, group(i + 1)], rl[one, :, group(i + 1)]
            else:
                v_then, l_then = v_right, l_right
            v_fore_own, l_fore_own = pltpu.roll(v, 1, 1), pltpu.roll(l, 1, 1)
            v_back_then, l_back_then = pltpu.roll(v_then, 127, 1), pltpu.roll(l_then, 127, 1)
            v_y = jnp.where(lane == 0, v_fore, v_fore_own) + jnp.where(lane == 127, v_back_then, v_back)
            l_y = jnp.where(lane == 0, l_fore, l_fore_own) + jnp.where(lane == 127, l_back_then, l_back)
            face = jnp.maximum(l, 0.0) * v + jnp.minimum(l, 0.0) * pltpu.roll(v, 47, 0)
            face = jnp.where(row == 47, 0.0, face)
            div = face - pltpu.roll(face, 1, 0)
            upwind = fx[one, :, group(i)] - fx[two, :, group(i)]
            sharpen = mark2 * (v * (1.0 - v) * (2.0 * v - 1.0))
            vol_out[0, :, group(i)] = v - 0.3 * (upwind + div) + 0.1 * (v_y - 2.0 * v) + sharpen
            l_z = jnp.where(row == 47, 0.0, pltpu.roll(l, 47, 0)) + jnp.where(row == 0, 0.0, pltpu.roll(l, 1, 0))
            l_x = rl[now, :, group(i)] + rl[two, :, group(i)]
            lft_out[0, :, group(i)] = l + 0.15 * (l_x + l_y + l_z - 6.0 * l)
            v, l = v_then, l_then
            v_fore, l_fore, v_back, l_back = v_fore_own, l_fore_own, v_back_then, l_back_then


def field_part(marks, hr, planes, cols, vol, lft, spd):
    vmem = pl.BlockSpec(memory_space=pltpu.VMEM)
    plane = pl.BlockSpec((1, 48, 1024), lambda t: (jnp.minimum(t, 7), 0, 0))
    out = pl.BlockSpec((1, 48, 1024), lambda t: (jnp.maximum(t - 1, 0), 0, 0))
    return pl.pallas_call(
        field_kernel,
        grid=(9,),
        out_shape=(jax.ShapeDtypeStruct((8, 48, 1024), F32),) * 2,
        in_specs=[pl.BlockSpec(memory_space=pltpu.SMEM), vmem, vmem, vmem, plane, plane, plane],
        out_specs=(out, out),
        scratch_shapes=[pltpu.VMEM((3, 48, 1024), F32)] * 3,
        compiler_params=pltpu.CompilerParams(vmem_limit_bytes=60 * 1024 * 1024),
        name="field_part",
    )(marks, hr, planes, cols, vol, lft, spd)


def on_device(eta_hat, phi_hat, zone_rows, zone_count, volume, lift, stream_speed, surface_blocks):
    hr, planes, cols = wave_part(zone_rows.T, zone_count, eta_hat, phi_hat, volume, lift, stream_speed)
    return field_part(surface_blocks, hr, planes, cols, volume, lift, stream_speed)


def solution(mesh):
    return jax.shard_map(
        on_device,
        mesh=mesh,
        in_specs=(
            P("stream", "girth"),
            P("stream", "girth"),
            P(),
            P("stream"),
            P("stream", None, "girth"),
            P("stream", None, "girth"),
            P("stream", None, "girth"),
            P("stream", None),
        ),
        out_specs=(P("stream", None, "girth"), P("stream", None, "girth")),
        check_vma=False,
    )
```

```python
import math

import jax
import jax.numpy as jnp
from jax import lax
from jax.experimental import pallas as pl
from jax.experimental.pallas import tpu as pltpu
from jax.sharding import PartitionSpec as P

F32 = jnp.float32
BF16 = jnp.bfloat16
MESH = pl.DeviceIdType.MESH
EXT = 1280

AG, RS, RZ, GA, ROWS, COLS, PLANES, RELAY = 0, 12, 24, 30, 33, 35, 37, 41
N_SEM = 46


def iota(shape, dim):
    return lax.broadcasted_iota(jnp.int32, shape, dim)


def quarter_turns(t):
    k = jnp.floor(t + 0.5)
    r = t - k
    r2 = r * r
    s = r * (
        1.5707963267949
        + r2 * (-0.645964097506 + r2 * (0.0796926262462 + r2 * (-0.00468175413532 + r2 * 0.000160441184787)))
    )
    c = 1.0 + r2 * (
        -1.23370055013617
        + r2 * (0.253669507901 + r2 * (-0.0208634807634 + r2 * (0.000919260274839 - r2 * 2.52020423731e-5)))
    )
    half = jnp.floor(k * 0.5)
    odd = (k - 2.0 * half) > 0.5
    sign = 1.0 - 2.0 * (half - 2.0 * jnp.floor(half * 0.5))
    return sign, odd, c, s


def cas_dcas(t):
    sign, odd, c, s = quarter_turns(t)
    plus, minus = c + s, c - s
    return sign * jnp.where(odd, minus, plus), sign * jnp.where(odd, -plus, minus)


def cos_sin(t):
    sign, odd, c, s = quarter_turns(t)
    return sign * jnp.where(odd, -s, c), sign * jnp.where(odd, c, s)


def split(value):
    hi = value.astype(BF16)
    return hi, (value - hi.astype(F32)).astype(BF16)


def dot(left, right):
    return jnp.dot(left, right, preferred_element_type=F32)


def dot3(left, right):
    (lh, ll), (rh, rl) = left, right
    return dot(lh, rh) + (dot(lh, rl) + dot(ll, rh))


def pick(index, values):
    out = values[-1]
    for i in range(len(values) - 2, -1, -1):
        out = jnp.where(index == i, values[i], out)
    return out


def wave_kernel(
    zr_hbm, zc_ref, marks, eta, phi_hbm, vol, lft, spd,
    vol_out, lft_out,
    hr, planes, cin, cmsg, ecol, vv, lv, sv, rv, rl, flux, ov, ol,
    ag, tab, ps, ob, nb, zs, zo, zn, xg, xp, e_hi, e_lo, perm, lhs, uu, hh, relay, zr_ref, phi,
    ssem, rsem, lsem, osem,
):
    s = lax.axis_index("stream")
    g = lax.axis_index("girth")
    zh, y, x = s // 16, (s // 4) % 4, s % 4

    def at(zh_, y_, x_):
        return (zh_ * 16 + y_ * 4 + x_, g)

    def turn(c, d):
        return lax.rem(c + d + 4, 4)

    def on_x(d):
        return at(zh, y, turn(x, d))

    def on_y(d):
        return at(zh, turn(y, d), x)

    def on_z(d):
        return at(turn(zh, d), y, x)

    fetched = [
        pltpu.make_async_copy(eta.at[:, pl.ds(0, 512)], ag.at[0, 0, 0], lsem.at[0]),
        pltpu.make_async_copy(eta.at[:, pl.ds(512, 512)], ag.at[1, 0, 0], lsem.at[1]),
        pltpu.make_async_copy(phi_hbm, phi, lsem.at[2]),
        pltpu.make_async_copy(zr_hbm, zr_ref, lsem.at[3]),
    ]
    edge_left, edge_right = pl.ds(0, 128), pl.ds(896, 128)
    fields = [
        pltpu.make_async_copy(vol.at[:, :, edge_right], ecol.at[0, 0], lsem.at[4]),
        pltpu.make_async_copy(lft.at[:, :, edge_right], ecol.at[0, 1], lsem.at[5]),
        pltpu.make_async_copy(vol.at[:, :, edge_left], ecol.at[1, 0], lsem.at[6]),
        pltpu.make_async_copy(lft.at[:, :, edge_left], ecol.at[1, 1], lsem.at[7]),
        pltpu.make_async_copy(vol, vv, lsem.at[8]),
        pltpu.make_async_copy(lft, lv, lsem.at[9]),
        pltpu.make_async_copy(spd, sv, lsem.at[10]),
    ]
    for c in fetched + fields:
        c.start()

    s_next = lax.rem(s + 1, 64)
    s_prev = lax.rem(s + 63, 64)

    def girth(j):
        return lax.rem(g + j, 4)

    targets = [on_x(1), on_x(-1), on_y(1), on_y(-1), on_z(1), on_z(-1)]
    targets += [(s, girth(j)) for j in (1, 2, 3)]
    targets += [(s_next, g), (s_prev, g), at(zh, 3 - y, 3 - x)]
    barrier = pltpu.get_barrier_semaphore()
    for device in targets:
        pl.semaphore_signal(barrier, inc=1, device_id=device, device_id_type=MESH)
    pl.semaphore_wait(barrier, len(targets))

    def copy(src, dst, index, device):
        return pltpu.make_async_remote_copy(
            src_ref=src, dst_ref=dst, send_sem=ssem.at[index], recv_sem=rsem.at[index],
            device_id=device, device_id_type=MESH,
        )

    sent = []

    def start(src, dst, index, device):
        c = copy(src, dst, index, device)
        c.start()
        sent.append(c)
        return c

    first = (on_x, on_y)
    second = (on_y, on_x)

    gat = {}
    for q in range(2):
        fetched[q].wait()
        gat[q, 0] = start(ag.at[q, 0, 0], ag.at[q, 0, 1], AG + 6 * q, first[q](1))
        gat[q, 1] = start(ag.at[q, 0, 0], ag.at[q, 0, 2], AG + 6 * q + 1, first[q](-1))
    high_edge = jnp.logical_and(x == 3, y == 3)
    low_edge = jnp.logical_and(x == 0, y == 0)

    up = [copy(f.at[7], relay.at[k], RELAY + k, on_z(1)) for k, f in enumerate((vol, spd))]
    across = copy(lft.at[7], relay.at[2], RELAY + 2, at(zh, 0, 0))
    upward = copy(relay.at[2], planes.at[2], PLANES + 2, on_z(1))
    down = copy(lft.at[0], relay.at[0], RELAY + 3, on_z(-1))

    @pl.when(high_edge)
    def _():
        for c in up:
            c.start()

    @pl.when(low_edge)
    def _():
        down.start()

    fetched[2].wait()
    kx_own = (s * 64 + iota((64, 1), 0)).astype(F32)
    fx_own = kx_own / 2048.0 - jnp.where(kx_own >= 2048.0, 2.0, 0.0)
    for q in range(2):
        cs = pl.ds(q * 512, 512)
        ky = (g * 1024 + q * 512 + iota((1, 512), 1)).astype(F32)
        fy = ky / 2048.0 - jnp.where(ky >= 2048.0, 2.0, 0.0)
        rad = jnp.sqrt(fx_own * fx_own + fy * fy)
        ag[q, 1, 0] = rad * jnp.tanh(2.0 * rad) * phi[:, cs]
        gat[q, 2] = start(ag.at[q, 1, 0], ag.at[q, 1, 1], AG + 6 * q + 2, first[q](1))
        gat[q, 3] = start(ag.at[q, 1, 0], ag.at[q, 1, 2], AG + 6 * q + 3, first[q](-1))

    fetched[3].wait()
    zr = zr_ref[...].astype(F32)
    lane64 = iota((8, 64), 1)
    lane256 = iota((1, 256), 1)
    slot = lane256 // 64
    rel = (0, 1, -1, 2)
    for q in range(2):
        here = x if q == 0 else y
        coords = [turn(here, d) for d in (0, -1, 1, 2)]
        if q == 0:
            slabs = [zh * 16 + y * 4 + c for c in coords]
        else:
            slabs = [zh * 16 + c * 4 + x for c in coords]
        kx = (pick(slot, slabs) * 64 + lane256 % 64).astype(F32)
        fx = kx / 2048.0 - jnp.where(kx >= 2048.0, 2.0, 0.0)
        for r in range(4):
            for z in range(4):
                zz = turn(zh, rel[z])
                want = zz * 16 + (turn(y, rel[r]) * 4 + x if q == 0 else y * 4 + turn(x, rel[r]))
                rows = jnp.sum(jnp.where(lane64 == want, zr, 0.0), axis=1, keepdims=True)
                t = rows * kx * (1.0 / 1024.0)
                even, odd = cas_dcas(t)
                tab[q, r, z, 0] = even
                tab[q, r, z, 1] = odd * fx

    for q in range(2):
        gat[q, 0].wait_recv()
        gat[q, 4] = start(ag.at[q, 0, 1], ag.at[q, 0, 3], AG + 6 * q + 4, first[q](1))
    for q in range(2):
        gat[q, 3].wait_recv()
        gat[q, 5] = start(ag.at[q, 1, 2], ag.at[q, 1, 3], AG + 6 * q + 5, first[q](-1))

    for c in fields[:4]:
        c.wait()
    lane = iota((48, 128), 1)
    for side, at_lane in ((0, 127), (1, 0)):
        packed = jnp.zeros((48, 128), F32)
        for f in range(2):
            for p in range(8):
                packed = jnp.where(lane == 8 * f + p, ecol[side, f, p, :, at_lane : at_lane + 1], packed)
        cmsg[side] = packed
    raw = [
        start(cmsg.at[0], cin.at[0], COLS, (s, girth(1))),
        start(cmsg.at[1], cin.at[1], COLS + 1, (s, girth(3))),
    ]

    def fill_e(i, _):
        row = pl.multiple_of(i * 32, 32)
        a = (row + iota((32, 1), 0)).astype(F32)
        c = iota((1, 512), 1).astype(F32)
        co, si = cos_sin(a * c * (1.0 / 128.0))
        for k, value in enumerate((co, si)):
            hi, lo = split(value)
            e_hi[pl.ds(row, 32), k * 512 : (k + 1) * 512] = hi
            e_lo[pl.ds(row, 32), k * 512 : (k + 1) * 512] = lo
        return 0

    lax.fori_loop(0, 16, fill_e, 0)

    def fill_p(i, _):
        row = pl.multiple_of(i * 32, 32)
        a = row + iota((32, 1024), 0)
        b = iota((32, 1024), 1)
        perm[pl.ds(row, 32), :] = jnp.where(a == 8 * (b % 128) + b // 128, 1.0, 0.0).astype(BF16)
        return 0

    lax.fori_loop(0, 32, fill_p, 0)

    near, mid = {}, {}
    for q in range(2):
        for k in (1, 2, 4, 5):
            gat[q, k].wait_recv()
        table = tab[q]
        both = split(table.reshape(256, 256))
        even = split(table[:, :, 0].reshape(128, 256))
        acc = dot3(both, split(ag[q, 0].reshape(256, 512)))
        ps[q, :, :, 0:2] = acc.reshape(4, 4, 2, 8, 512)
        acc = dot3(even, split(ag[q, 1].reshape(256, 512)))
        ps[q, :, :, 2] = acc.reshape(4, 4, 8, 512)
        b = RS + 6 * q
        right, left = second[q](1), second[q](-1)
        near[q, 0] = start(ps.at[q, 3, pl.ds(0, 2)], ob.at[q, 0], b, right)
        near[q, 1] = start(ps.at[q, 3, pl.ds(2, 2)], ob.at[q, 1], b + 1, left)
        near[q, 2] = start(ps.at[q, 1, pl.ds(2, 2)], nb.at[q, 0, pl.ds(2, 2)], b + 2, right)
        near[q, 3] = start(ps.at[q, 2, pl.ds(0, 2)], nb.at[q, 1, pl.ds(0, 2)], b + 3, left)
    for q in range(2):
        b = RS + 6 * q
        right, left = second[q](1), second[q](-1)
        near[q, 0].wait_recv()
        ps[q, 1, 0:2] = ps[q, 1, 0:2] + ob[q, 0]
        near[q, 4] = start(ps.at[q, 1, pl.ds(0, 2)], nb.at[q, 0, pl.ds(0, 2)], b + 4, right)
        near[q, 1].wait_recv()
        ps[q, 2, 2:4] = ps[q, 2, 2:4] + ob[q, 1]
        near[q, 5] = start(ps.at[q, 2, pl.ds(2, 2)], nb.at[q, 1, pl.ds(2, 2)], b + 5, left)

    onward = [copy(f.at[7], planes.at[k], PLANES + k, (s_next, g)) for k, f in enumerate((vol, spd, lft))]
    onward_far = [copy(relay.at[k], planes.at[k], PLANES + k, at(zh, 0, 0)) for k in range(2)]
    backward = copy(lft.at[0], planes.at[3], PLANES + 3, (s_prev, g))
    backward_far = copy(relay.at[0], planes.at[3], PLANES + 3, at(zh, 3, 3))

    @pl.when(high_edge)
    def _():
        across.start()

    @pl.when(jnp.logical_not(high_edge))
    def _():
        for c in onward:
            c.start()

    @pl.when(jnp.logical_not(low_edge))
    def _():
        backward.start()

    right, left = on_z(1), on_z(-1)
    for q in range(2):
        for k in (2, 3, 4, 5):
            near[q, k].wait_recv()
        zs[q] = ps[q, 0] + nb[q, 0] + nb[q, 1]
        b = RZ + 3 * q
        ahead, back = (right, left) if q == 0 else (left, right)
        fore, aft = (1, 2) if q == 0 else (2, 1)
        mid[q, 0] = start(zs.at[q, 3], zo.at[q], b, ahead)
        mid[q, 1] = start(zs.at[q, aft], zn.at[q, 1], b + 1, back)
    for q in range(2):
        b = RZ + 3 * q
        ahead = right if q == 0 else left
        fore = 1 if q == 0 else 2
        mid[q, 0].wait_recv()
        zs[q, fore] = zs[q, fore] + zo[q]
        mid[q, 2] = start(zs.at[q, fore], zn.at[q, 0], b + 2, ahead)
    for q in range(2):
        mid[q, 1].wait_recv()
        mid[q, 2].wait_recv()
        xp[:, :, q * 512 : (q + 1) * 512] = zs[q, 0] + zn[q, 0] + zn[q, 1]

    @pl.when(high_edge)
    def _():
        for k in range(2):
            up[k].wait_recv()
            onward_far[k].start()

    @pl.when(low_edge)
    def _():
        down.wait_recv()
        backward_far.start()
        across.wait_recv()
        upward.start()

    hi, lo = split(xp[...].reshape(24, 1024))
    moved = dot(hi, perm[...]) + dot(lo, perm[...])
    moved = moved.reshape(3, 8, 1024)
    xg[g] = moved
    last = []
    for j in (1, 2, 3):
        last.append(start(xg.at[g], xg.at[g], GA + j - 1, (s, girth(j))))
    for c in last:
        c.wait_recv()

    for gg in range(4):
        os = slice(128 * gg, 128 * (gg + 1))
        for b in range(8):
            ks = slice(128 * b, 128 * (b + 1))
            ky = (1024 * gg + b + 8 * iota((1, 128), 1)).astype(F32)
            fy = ky * (1.0 / 2048.0) - (2.0 if gg >= 2 else 0.0)
            top = xg[gg, 0, :, ks]
            lhs[b, 0:8, os] = top
            lhs[b, 8:16, os] = xg[gg, 1, :, ks]
            lhs[b, 16:24, os] = xg[gg, 2, :, ks]
            lhs[b, 24:32, os] = top * fy
    uu[...] = dot3(split(lhs[...].reshape(256, 512)), (e_hi[...], e_lo[...])).reshape(8, 32, 1024)

    places = [(2 * g - 1, 384)] + [(2 * g + i // 4, 128 * (i % 4)) for i in range(8)] + [(2 * g + 2, 0)]
    b8 = iota((8, 128), 0)
    for i, (block, c0) in enumerate(places):
        c = c0 + iota((8, 128), 1)
        t = (b8 * c).astype(F32) * (1.0 / 1024.0) + (b8 * block).astype(F32) * 0.5
        even, odd = cas_dcas(t)
        out = [jnp.zeros((8, 128), F32) for _ in range(4)]
        for b in range(8):
            ev, od = even[b : b + 1], odd[b : b + 1]
            for k in range(4):
                re = uu[b, 8 * k : 8 * k + 8, c0 : c0 + 128]
                im = uu[b, 8 * k : 8 * k + 8, 512 + c0 : 512 + c0 + 128]
                out[k] = out[k] + (re * ev + im * od if k < 3 else re * od - im * ev)
        cs = slice(128 * i, 128 * (i + 1))
        for k in range(4):
            hh[k, :, cs] = out[k]

    plane = iota((8, 128), 0).astype(F32)
    count = jnp.full((8, 128), zc_ref[0].astype(F32))
    q_ = jnp.minimum((plane + 0.5) / count, 1.0)
    w = 1.0 - (jnp.exp(q_ * q_ * q_ * jnp.sqrt(q_)) - 1.0) / (math.e - 1.0)
    w = jnp.where(plane < count, w, 0.0)
    for i in range(10):
        cs = slice(128 * i, 128 * (i + 1))
        height, tilt_x, lift, tilt_y = (hh[k, :, cs] for k in range(4))
        rise = (1.0 + tilt_x * tilt_x + tilt_y * tilt_y) * lift
        parts = (0.5 + 8.0 * height, jnp.exp(-0.5 * height), w * rise, w)
        for p in range(8):
            for k in range(4):
                hr[p, k : k + 1, cs] = parts[k][p : p + 1]

    rows = [
        start(hr.at[7], hr.at[8], ROWS, (s_next, g)),
        start(hr.at[0], hr.at[9], ROWS + 1, (s_prev, g)),
    ]

    for c in fields[4:]:
        c.wait()
    level8 = iota((48, 128), 0).astype(F32) - 23.5
    rise_z = jnp.exp(level8 * 0.0625)
    row = iota((48, 128), 0)

    def group(i):
        return slice(128 * i, 128 * (i + 1))

    def surface(plane, i):
        return [hr[plane, k : k + 1, group(i)] for k in range(4)]

    def relax_v(v, here):
        goal = jnp.clip(here[0] - level8, 0.0, 1.0)
        return here[3] * goal + (1.0 - here[3]) * v

    def relax_l(l, here):
        return here[2] * jnp.minimum(rise_z * here[1], 1.0) + (1.0 - here[3]) * l

    def relax_plane(p, _):
        for i in range(8):
            here = surface(p, i + 1)
            v = relax_v(vv[p, :, group(i)], here)
            rv[p, :, group(i)] = v
            flux[p + 1, :, group(i)] = sv[p, :, group(i)] * v
            rl[p + 1, :, group(i)] = relax_l(lv[p, :, group(i)], here)
        return 0

    lax.fori_loop(0, 8, relax_plane, 0)
    for c in raw:
        c.wait_recv()

    def put_out(u):
        return (
            pltpu.make_async_copy(ov.at[u], vol_out.at[u], osem.at[0, u]),
            pltpu.make_async_copy(ol.at[u], lft_out.at[u], osem.at[1, u]),
        )

    def step(n, _):
        u = lax.rem(n + 1, 8)
        mark2 = jnp.concatenate(
            [jnp.full((8, 128), 2.0 * marks[u, k].astype(F32), F32) for k in range(6)], axis=0
        )

        def edge(side, f):
            return jnp.sum(jnp.where(lane == u + 8 * f, cin[side], 0.0), axis=1, keepdims=True)

        here = surface(u, 0)
        v_left = jnp.where(g > 0, relax_v(edge(0, 0), here), 0.0)
        l_left = jnp.where(g > 0, relax_l(edge(0, 1), here), 0.0)
        here = surface(u, 9)
        v_right = jnp.where(g < 3, relax_v(edge(1, 0), here), 0.0)
        l_right = jnp.where(g < 3, relax_l(edge(1, 1), here), 0.0)
        v = rv[u, :, group(0)]
        l = rl[u + 1, :, group(0)]
        v_fore, l_fore = pltpu.roll(v_left, 1, 1), pltpu.roll(l_left, 1, 1)
        v_back, l_back = pltpu.roll(v, 127, 1), pltpu.roll(l, 127, 1)
        for i in range(8):
            if i < 7:
                v_then, l_then = rv[u, :, group(i + 1)], rl[u + 1, :, group(i + 1)]
            else:
                v_then, l_then = v_right, l_right
            v_fore_own, l_fore_own = pltpu.roll(v, 1, 1), pltpu.roll(l, 1, 1)
            v_back_then, l_back_then = pltpu.roll(v_then, 127, 1), pltpu.roll(l_then, 127, 1)
            v_y = jnp.where(lane == 0, v_fore, v_fore_own) + jnp.where(lane == 127, v_back_then, v_back)
            l_y = jnp.where(lane == 0, l_fore, l_fore_own) + jnp.where(lane == 127, l_back_then, l_back)
            face = jnp.maximum(l, 0.0) * v + jnp.minimum(l, 0.0) * pltpu.roll(v, 47, 0)
            face = jnp.where(row == 47, 0.0, face)
            div = face - pltpu.roll(face, 1, 0)
            upwind = flux[u + 1, :, group(i)] - flux[u, :, group(i)]
            sharpen = mark2 * (v * (1.0 - v) * (2.0 * v - 1.0))
            ov[u, :, group(i)] = v - 0.3 * (upwind + div) + 0.1 * (v_y - 2.0 * v) + sharpen
            l_z = jnp.where(row == 47, 0.0, pltpu.roll(l, 47, 0)) + jnp.where(row == 0, 0.0, pltpu.roll(l, 1, 0))
            l_x = rl[u + 2, :, group(i)] + rl[u, :, group(i)]
            ol[u, :, group(i)] = l + 0.15 * (l_x + l_y + l_z - 6.0 * l)
            v, l = v_then, l_then
            v_fore, l_fore, v_back, l_back = v_fore_own, l_fore_own, v_back_then, l_back_then
        for c in put_out(u):
            c.start()
        return 0

    lax.fori_loop(0, 6, step, 0)
    for c in rows + onward + [backward]:
        c.wait_recv()
    for i in range(8):
        here = surface(8, i + 1)
        v = relax_v(planes[0, :, group(i)], here)
        l = relax_l(planes[2, :, group(i)], here)
        flux[0, :, group(i)] = jnp.where(s > 0, planes[1, :, group(i)] * v, 0.0)
        rl[0, :, group(i)] = jnp.where(s > 0, l, 0.0)
        l = relax_l(planes[3, :, group(i)], surface(9, i + 1))
        rl[9, :, group(i)] = jnp.where(s < 63, l, 0.0)
    lax.fori_loop(6, 8, step, 0)

    for c in sent:
        c.wait_send()

    @pl.when(high_edge)
    def _():
        for c in up + onward_far + [across]:
            c.wait_send()

    @pl.when(jnp.logical_not(high_edge))
    def _():
        for c in onward:
            c.wait_send()

    @pl.when(low_edge)
    def _():
        down.wait_send()
        upward.wait_send()
        backward_far.wait_send()

    @pl.when(jnp.logical_not(low_edge))
    def _():
        backward.wait_send()

    for u in range(8):
        for c in put_out(u):
            c.wait()


def pass_on(a, b, a_out, b_out, held, sem, sem_out):
    pairs = [(k, i) for i in range(8) for k in range(2)]
    loads = [pltpu.make_async_copy((a, b)[k].at[i], held.at[k, i], sem.at[k, i]) for k, i in pairs]
    stores = [pltpu.make_async_copy(held.at[k, i], (a_out, b_out)[k].at[i], sem_out.at[k, i]) for k, i in pairs]
    for c in loads:
        c.start()
    for load, store in zip(loads, stores):
        load.wait()
        store.start()
    for c in stores:
        c.wait()


def on_device(eta_hat, phi_hat, zone_rows, zone_count, volume, lift, stream_speed, surface_blocks):
    smem = pl.BlockSpec(memory_space=pltpu.SMEM)
    anyw = pl.BlockSpec(memory_space=pl.ANY)
    field = jax.ShapeDtypeStruct((8, 48, 1024), F32)
    results = pl.pallas_call(
        wave_kernel,
        out_shape=(field, field),
        in_specs=[anyw, smem, smem, anyw, anyw, anyw, anyw, anyw],
        out_specs=(anyw, anyw),
        scratch_shapes=[
            pltpu.VMEM((10, 4, EXT), F32),
            pltpu.VMEM((4, 48, 1024), F32),
            pltpu.VMEM((2, 48, 128), F32),
            pltpu.VMEM((2, 48, 128), F32),
            pltpu.VMEM((2, 2, 8, 48, 128), F32),
            pltpu.VMEM((8, 48, 1024), F32),
            pltpu.VMEM((8, 48, 1024), F32),
            pltpu.VMEM((8, 48, 1024), F32),
            pltpu.VMEM((8, 48, 1024), F32),
            pltpu.VMEM((10, 48, 1024), F32),
            pltpu.VMEM((9, 48, 1024), F32),
            pltpu.VMEM((8, 48, 1024), F32),
            pltpu.VMEM((8, 48, 1024), F32),
            pltpu.VMEM((2, 2, 4, 64, 512), F32),
            pltpu.VMEM((2, 4, 4, 2, 8, 256), F32),
            pltpu.VMEM((2, 4, 4, 3, 8, 512), F32),
            pltpu.VMEM((2, 2, 2, 3, 8, 512), F32),
            pltpu.VMEM((2, 2, 4, 3, 8, 512), F32),
            pltpu.VMEM((2, 4, 3, 8, 512), F32),
            pltpu.VMEM((2, 3, 8, 512), F32),
            pltpu.VMEM((2, 2, 3, 8, 512), F32),
            pltpu.VMEM((4, 3, 8, 1024), F32),
            pltpu.VMEM((3, 8, 1024), F32),
            pltpu.VMEM((512, 1024), BF16),
            pltpu.VMEM((512, 1024), BF16),
            pltpu.VMEM((1024, 1024), BF16),
            pltpu.VMEM((8, 32, 512), F32),
            pltpu.VMEM((8, 32, 1024), F32),
            pltpu.VMEM((4, 8, EXT), F32),
            pltpu.VMEM((3, 48, 1024), F32),
            pltpu.VMEM((8, 64), jnp.int32),
            pltpu.VMEM((64, 1024), F32),
            pltpu.SemaphoreType.DMA((N_SEM,)),
            pltpu.SemaphoreType.DMA((N_SEM,)),
            pltpu.SemaphoreType.DMA((11,)),
            pltpu.SemaphoreType.DMA((2, 8)),
        ],
        compiler_params=pltpu.CompilerParams(
            collective_id=0, has_side_effects=True, vmem_limit_bytes=60 * 1024 * 1024
        ),
        name="wave_part",
    )(zone_rows.T, zone_count, surface_blocks, eta_hat, phi_hat, volume, lift, stream_speed)
    return pl.pallas_call(
        pass_on,
        out_shape=(field, field),
        in_specs=[anyw, anyw],
        out_specs=(anyw, anyw),
        scratch_shapes=[pltpu.VMEM((2, 8, 48, 1024), F32), pltpu.SemaphoreType.DMA((2, 8)), pltpu.SemaphoreType.DMA((2, 8))],
        compiler_params=pltpu.CompilerParams(vmem_limit_bytes=60 * 1024 * 1024),
        name="pass_on",
    )(*results)


def solution(mesh):
    return jax.shard_map(
        on_device,
        mesh=mesh,
        in_specs=(
            P("stream", "girth"),
            P("stream", "girth"),
            P(),
            P("stream"),
            P("stream", None, "girth"),
            P("stream", None, "girth"),
            P("stream", None, "girth"),
            P("stream", None),
        ),
        out_specs=(P("stream", None, "girth"), P("stream", None, "girth")),
        check_vma=False,
    )
```

```python
import math

import jax
import jax.numpy as jnp
from jax import lax
from jax.experimental import pallas as pl
from jax.experimental.pallas import tpu as pltpu
from jax.sharding import PartitionSpec as P

F32 = jnp.float32
BF16 = jnp.bfloat16
MESH = pl.DeviceIdType.MESH
EXT = 1280

AG, RS, RZ, GA, ROWS, COLS, PLANES, RELAY = 0, 12, 24, 30, 33, 35, 37, 42
N_SEM = 47


def iota(shape, dim):
    return lax.broadcasted_iota(jnp.int32, shape, dim)


def quarter_turns(t):
    k = jnp.floor(t + 0.5)
    r = t - k
    r2 = r * r
    s = r * (
        1.5707963267949
        + r2 * (-0.645964097506 + r2 * (0.0796926262462 + r2 * (-0.00468175413532 + r2 * 0.000160441184787)))
    )
    c = 1.0 + r2 * (
        -1.23370055013617
        + r2 * (0.253669507901 + r2 * (-0.0208634807634 + r2 * (0.000919260274839 - r2 * 2.52020423731e-5)))
    )
    half = jnp.floor(k * 0.5)
    odd = (k - 2.0 * half) > 0.5
    sign = 1.0 - 2.0 * (half - 2.0 * jnp.floor(half * 0.5))
    return sign, odd, c, s


def cas_dcas(t):
    sign, odd, c, s = quarter_turns(t)
    plus, minus = c + s, c - s
    return sign * jnp.where(odd, minus, plus), sign * jnp.where(odd, -plus, minus)


def cos_sin(t):
    sign, odd, c, s = quarter_turns(t)
    return sign * jnp.where(odd, -s, c), sign * jnp.where(odd, c, s)


def split(value):
    hi = value.astype(BF16)
    return hi, (value - hi.astype(F32)).astype(BF16)


def dot(left, right):
    return jnp.dot(left, right, preferred_element_type=F32)


def dot3(left, right):
    (lh, ll), (rh, rl) = left, right
    return dot(lh, rh) + (dot(lh, rl) + dot(ll, rh))


def pick(index, values):
    out = values[-1]
    for i in range(len(values) - 2, -1, -1):
        out = jnp.where(index == i, values[i], out)
    return out


def wave_kernel(
    zr_hbm, zc_ref, marks, eta, phi_hbm, vol, lft, spd,
    vol_out, lft_out,
    hr, planes, cin, cmsg, ecol, vv, lv, sv, rv, rl, flux, ov, ol,
    ag, tab, ps, ob, nb, zs, zo, zn, xg, xp, e_hi, e_lo, perm, lhs, uu, hh, relay, zr_ref, phi,
    ssem, rsem, lsem, osem,
):
    s = lax.axis_index("stream")
    g = lax.axis_index("girth")
    zh, y, x = s // 16, (s // 4) % 4, s % 4

    def at(zh_, y_, x_):
        return (zh_ * 16 + y_ * 4 + x_, g)

    def turn(c, d):
        return lax.rem(c + d + 4, 4)

    def on_x(d):
        return at(zh, y, turn(x, d))

    def on_y(d):
        return at(zh, turn(y, d), x)

    def on_z(d):
        return at(turn(zh, d), y, x)

    fetched = [
        pltpu.make_async_copy(eta.at[:, pl.ds(0, 512)], ag.at[0, 0, 0], lsem.at[0]),
        pltpu.make_async_copy(eta.at[:, pl.ds(512, 512)], ag.at[1, 0, 0], lsem.at[1]),
        pltpu.make_async_copy(phi_hbm, phi, lsem.at[2]),
        pltpu.make_async_copy(zr_hbm, zr_ref, lsem.at[3]),
    ]
    edge_left, edge_right = pl.ds(0, 128), pl.ds(896, 128)
    fields = [
        pltpu.make_async_copy(vol.at[:, :, edge_right], ecol.at[0, 0], lsem.at[4]),
        pltpu.make_async_copy(lft.at[:, :, edge_right], ecol.at[0, 1], lsem.at[5]),
        pltpu.make_async_copy(vol.at[:, :, edge_left], ecol.at[1, 0], lsem.at[6]),
        pltpu.make_async_copy(lft.at[:, :, edge_left], ecol.at[1, 1], lsem.at[7]),
        pltpu.make_async_copy(vol, vv, lsem.at[8]),
        pltpu.make_async_copy(lft, lv, lsem.at[9]),
        pltpu.make_async_copy(spd, sv, lsem.at[10]),
    ]
    for c in fetched:
        c.start()

    s_next = lax.rem(s + 1, 64)
    s_prev = lax.rem(s + 63, 64)

    def girth(j):
        return lax.rem(g + j, 4)

    targets = [on_x(1), on_x(-1), on_y(1), on_y(-1), on_z(1), on_z(-1)]
    targets += [(s, girth(j)) for j in (1, 2, 3)]
    targets += [(s_next, g), (s_prev, g), at(zh, 3 - y, 3 - x)]
    barrier = pltpu.get_barrier_semaphore()
    for device in targets:
        pl.semaphore_signal(barrier, inc=1, device_id=device, device_id_type=MESH)
    pl.semaphore_wait(barrier, len(targets))

    def copy(src, dst, index, device):
        return pltpu.make_async_remote_copy(
            src_ref=src, dst_ref=dst, send_sem=ssem.at[index], recv_sem=rsem.at[index],
            device_id=device, device_id_type=MESH,
        )

    sent = []

    def start(src, dst, index, device):
        c = copy(src, dst, index, device)
        c.start()
        sent.append(c)
        return c

    first = (on_x, on_y)
    second = (on_y, on_x)

    gat = {}
    for q in range(2):
        fetched[q].wait()
        gat[q, 0] = start(ag.at[q, 0, 0], ag.at[q, 0, 1], AG + 6 * q, first[q](1))
        gat[q, 1] = start(ag.at[q, 0, 0], ag.at[q, 0, 2], AG + 6 * q + 1, first[q](-1))
    high_edge = jnp.logical_and(x == 3, y == 3)
    low_edge = jnp.logical_and(x == 0, y == 0)

    def piece(ref, k):
        return ref.at[k] if k < 2 else ref.at[2, pl.ds(0, 24) if k == 3 else pl.ds(24, 24)]

    def own(k):
        return (vol.at[7], spd.at[7], lft.at[7, pl.ds(24, 24)], lft.at[7, pl.ds(0, 24)])[k]

    up = [copy(own(k), piece(relay, k), RELAY + k, on_z(1)) for k in (0, 1, 3)]
    across = copy(own(2), piece(relay, 2), RELAY + 2, at(zh, 0, 0))
    upward = copy(piece(relay, 2), piece(planes, 2), PLANES + 2, on_z(1))
    down = copy(lft.at[0], relay.at[0], RELAY + 4, on_z(-1))

    @pl.when(high_edge)
    def _():
        for c in up:
            c.start()

    @pl.when(low_edge)
    def _():
        down.start()

    fetched[2].wait()
    kx_own = (s * 64 + iota((64, 1), 0)).astype(F32)
    fx_own = kx_own / 2048.0 - jnp.where(kx_own >= 2048.0, 2.0, 0.0)
    for q in range(2):
        cs = pl.ds(q * 512, 512)
        ky = (g * 1024 + q * 512 + iota((1, 512), 1)).astype(F32)
        fy = ky / 2048.0 - jnp.where(ky >= 2048.0, 2.0, 0.0)
        rad = jnp.sqrt(fx_own * fx_own + fy * fy)
        ag[q, 1, 0] = rad * jnp.tanh(2.0 * rad) * phi[:, cs]
        gat[q, 2] = start(ag.at[q, 1, 0], ag.at[q, 1, 1], AG + 6 * q + 2, first[q](1))
        gat[q, 3] = start(ag.at[q, 1, 0], ag.at[q, 1, 2], AG + 6 * q + 3, first[q](-1))

    fetched[3].wait()
    zr = zr_ref[...].astype(F32)
    lane64 = iota((8, 64), 1)
    lane256 = iota((1, 256), 1)
    slot = lane256 // 64
    rel = (0, 1, -1, 2)
    for q in range(2):
        here = x if q == 0 else y
        coords = [turn(here, d) for d in (0, -1, 1, 2)]
        if q == 0:
            slabs = [zh * 16 + y * 4 + c for c in coords]
        else:
            slabs = [zh * 16 + c * 4 + x for c in coords]
        kx = (pick(slot, slabs) * 64 + lane256 % 64).astype(F32)
        fx = kx / 2048.0 - jnp.where(kx >= 2048.0, 2.0, 0.0)
        for r in range(4):
            for z in range(4):
                zz = turn(zh, rel[z])
                want = zz * 16 + (turn(y, rel[r]) * 4 + x if q == 0 else y * 4 + turn(x, rel[r]))
                rows = jnp.sum(jnp.where(lane64 == want, zr, 0.0), axis=1, keepdims=True)
                t = rows * kx * (1.0 / 1024.0)
                even, odd = cas_dcas(t)
                tab[q, r, z, 0] = even
                tab[q, r, z, 1] = odd * fx

    for q in range(2):
        gat[q, 0].wait_recv()
        gat[q, 4] = start(ag.at[q, 0, 1], ag.at[q, 0, 3], AG + 6 * q + 4, first[q](1))
    for q in range(2):
        gat[q, 3].wait_recv()
        gat[q, 5] = start(ag.at[q, 1, 2], ag.at[q, 1, 3], AG + 6 * q + 5, first[q](-1))

    def fill_e(i, _):
        row = pl.multiple_of(i * 32, 32)
        a = (row + iota((32, 1), 0)).astype(F32)
        c = iota((1, 512), 1).astype(F32)
        co, si = cos_sin(a * c * (1.0 / 128.0))
        for k, value in enumerate((co, si)):
            hi, lo = split(value)
            e_hi[pl.ds(row, 32), k * 512 : (k + 1) * 512] = hi
            e_lo[pl.ds(row, 32), k * 512 : (k + 1) * 512] = lo
        return 0

    lax.fori_loop(0, 16, fill_e, 0)

    def fill_p(i, _):
        row = pl.multiple_of(i * 32, 32)
        a = row + iota((32, 1024), 0)
        b = iota((32, 1024), 1)
        perm[pl.ds(row, 32), :] = jnp.where(a == 8 * (b % 128) + b // 128, 1.0, 0.0).astype(BF16)
        return 0

    lax.fori_loop(0, 32, fill_p, 0)

    near, mid = {}, {}
    for q in range(2):
        for k in (1, 2, 4, 5):
            gat[q, k].wait_recv()
        table = tab[q]
        both = split(table.reshape(256, 256))
        even = split(table[:, :, 0].reshape(128, 256))
        acc = dot3(both, split(ag[q, 0].reshape(256, 512)))
        ps[q, :, :, 0:2] = acc.reshape(4, 4, 2, 8, 512)
        acc = dot3(even, split(ag[q, 1].reshape(256, 512)))
        ps[q, :, :, 2] = acc.reshape(4, 4, 8, 512)
        b = RS + 6 * q
        right, left = second[q](1), second[q](-1)
        near[q, 0] = start(ps.at[q, 3, pl.ds(0, 2)], ob.at[q, 0], b, right)
        near[q, 1] = start(ps.at[q, 3, pl.ds(2, 2)], ob.at[q, 1], b + 1, left)
        near[q, 2] = start(ps.at[q, 1, pl.ds(2, 2)], nb.at[q, 0, pl.ds(2, 2)], b + 2, right)
        near[q, 3] = start(ps.at[q, 2, pl.ds(0, 2)], nb.at[q, 1, pl.ds(0, 2)], b + 3, left)
    for q in range(2):
        b = RS + 6 * q
        right, left = second[q](1), second[q](-1)
        near[q, 0].wait_recv()
        ps[q, 1, 0:2] = ps[q, 1, 0:2] + ob[q, 0]
        near[q, 4] = start(ps.at[q, 1, pl.ds(0, 2)], nb.at[q, 0, pl.ds(0, 2)], b + 4, right)
        near[q, 1].wait_recv()
        ps[q, 2, 2:4] = ps[q, 2, 2:4] + ob[q, 1]
        near[q, 5] = start(ps.at[q, 2, pl.ds(2, 2)], nb.at[q, 1, pl.ds(2, 2)], b + 5, left)

    for c in fields:
        c.start()
    for c in fields[:4]:
        c.wait()
    lane = iota((48, 128), 1)
    for side, at_lane in ((0, 127), (1, 0)):
        packed = jnp.zeros((48, 128), F32)
        for f in range(2):
            for p in range(8):
                packed = jnp.where(lane == 8 * f + p, ecol[side, f, p, :, at_lane : at_lane + 1], packed)
        cmsg[side] = packed
    raw = [
        start(cmsg.at[0], cin.at[0], COLS, (s, girth(1))),
        start(cmsg.at[1], cin.at[1], COLS + 1, (s, girth(3))),
    ]

    onward = [copy(own(k), piece(planes, k), PLANES + k, (s_next, g)) for k in range(4)]
    onward_far = [copy(piece(relay, k), piece(planes, k), PLANES + k, at(zh, 0, 0)) for k in (0, 1, 3)]
    backward = copy(lft.at[0], planes.at[3], PLANES + 4, (s_prev, g))
    backward_far = copy(relay.at[0], planes.at[3], PLANES + 4, at(zh, 3, 3))

    @pl.when(high_edge)
    def _():
        across.start()

    @pl.when(jnp.logical_not(high_edge))
    def _():
        for c in onward:
            c.start()

    @pl.when(jnp.logical_not(low_edge))
    def _():
        backward.start()

    right, left = on_z(1), on_z(-1)
    for q in range(2):
        for k in (2, 3, 4, 5):
            near[q, k].wait_recv()
        zs[q] = ps[q, 0] + nb[q, 0] + nb[q, 1]
        b = RZ + 3 * q
        ahead, back = (right, left) if q == 0 else (left, right)
        fore, aft = (1, 2) if q == 0 else (2, 1)
        mid[q, 0] = start(zs.at[q, 3], zo.at[q], b, ahead)
        mid[q, 1] = start(zs.at[q, aft], zn.at[q, 1], b + 1, back)
    for q in range(2):
        b = RZ + 3 * q
        ahead = right if q == 0 else left
        fore = 1 if q == 0 else 2
        mid[q, 0].wait_recv()
        zs[q, fore] = zs[q, fore] + zo[q]
        mid[q, 2] = start(zs.at[q, fore], zn.at[q, 0], b + 2, ahead)
    for q in range(2):
        mid[q, 1].wait_recv()
        mid[q, 2].wait_recv()
        xp[:, :, q * 512 : (q + 1) * 512] = zs[q, 0] + zn[q, 0] + zn[q, 1]

    @pl.when(high_edge)
    def _():
        for c, d in zip(up, onward_far):
            c.wait_recv()
            d.start()

    @pl.when(low_edge)
    def _():
        down.wait_recv()
        backward_far.start()

    hi, lo = split(xp[...].reshape(24, 1024))
    moved = dot(hi, perm[...]) + dot(lo, perm[...])
    moved = moved.reshape(3, 8, 1024)
    xg[g] = moved
    last = []
    for j in (1, 2, 3):
        last.append(start(xg.at[g], xg.at[g], GA + j - 1, (s, girth(j))))
    for c in last:
        c.wait_recv()

    @pl.when(low_edge)
    def _():
        across.wait_recv()
        upward.start()

    for gg in range(4):
        os = slice(128 * gg, 128 * (gg + 1))
        for b in range(8):
            ks = slice(128 * b, 128 * (b + 1))
            ky = (1024 * gg + b + 8 * iota((1, 128), 1)).astype(F32)
            fy = ky * (1.0 / 2048.0) - (2.0 if gg >= 2 else 0.0)
            top = xg[gg, 0, :, ks]
            lhs[b, 0:8, os] = top
            lhs[b, 8:16, os] = xg[gg, 1, :, ks]
            lhs[b, 16:24, os] = xg[gg, 2, :, ks]
            lhs[b, 24:32, os] = top * fy
    uu[...] = dot3(split(lhs[...].reshape(256, 512)), (e_hi[...], e_lo[...])).reshape(8, 32, 1024)

    places = [(2 * g - 1, 384)] + [(2 * g + i // 4, 128 * (i % 4)) for i in range(8)] + [(2 * g + 2, 0)]
    b8 = iota((8, 128), 0)
    for i, (block, c0) in enumerate(places):
        c = c0 + iota((8, 128), 1)
        t = (b8 * c).astype(F32) * (1.0 / 1024.0) + (b8 * block).astype(F32) * 0.5
        even, odd = cas_dcas(t)
        out = [jnp.zeros((8, 128), F32) for _ in range(4)]
        for b in range(8):
            ev, od = even[b : b + 1], odd[b : b + 1]
            for k in range(4):
                re = uu[b, 8 * k : 8 * k + 8, c0 : c0 + 128]
                im = uu[b, 8 * k : 8 * k + 8, 512 + c0 : 512 + c0 + 128]
                out[k] = out[k] + (re * ev + im * od if k < 3 else re * od - im * ev)
        cs = slice(128 * i, 128 * (i + 1))
        for k in range(4):
            hh[k, :, cs] = out[k]

    plane = iota((8, 128), 0).astype(F32)
    count = jnp.full((8, 128), zc_ref[0].astype(F32))
    q_ = jnp.minimum((plane + 0.5) / count, 1.0)
    w = 1.0 - (jnp.exp(q_ * q_ * q_ * jnp.sqrt(q_)) - 1.0) / (math.e - 1.0)
    w = jnp.where(plane < count, w, 0.0)
    for i in range(10):
        cs = slice(128 * i, 128 * (i + 1))
        height, tilt_x, lift, tilt_y = (hh[k, :, cs] for k in range(4))
        rise = (1.0 + tilt_x * tilt_x + tilt_y * tilt_y) * lift
        parts = (0.5 + 8.0 * height, jnp.exp(-0.5 * height), w * rise, w)
        for p in range(8):
            for k in range(4):
                hr[p, k : k + 1, cs] = parts[k][p : p + 1]

    rows = [
        start(hr.at[7], hr.at[8], ROWS, (s_next, g)),
        start(hr.at[0], hr.at[9], ROWS + 1, (s_prev, g)),
    ]

    for c in fields[4:]:
        c.wait()
    level8 = iota((48, 128), 0).astype(F32) - 23.5
    rise_z = jnp.exp(level8 * 0.0625)
    row = iota((48, 128), 0)

    def group(i):
        return slice(128 * i, 128 * (i + 1))

    def surface(plane, i):
        return [hr[plane, k : k + 1, group(i)] for k in range(4)]

    def relax_v(v, here):
        goal = jnp.clip(here[0] - level8, 0.0, 1.0)
        return here[3] * goal + (1.0 - here[3]) * v

    def relax_l(l, here):
        return here[2] * jnp.minimum(rise_z * here[1], 1.0) + (1.0 - here[3]) * l

    def relax_plane(p, _):
        for i in range(8):
            here = surface(p, i + 1)
            v = relax_v(vv[p, :, group(i)], here)
            rv[p, :, group(i)] = v
            flux[p + 1, :, group(i)] = sv[p, :, group(i)] * v
            rl[p + 1, :, group(i)] = relax_l(lv[p, :, group(i)], here)
        return 0

    lax.fori_loop(0, 8, relax_plane, 0)
    for c in raw:
        c.wait_recv()

    def put_out(u):
        return (
            pltpu.make_async_copy(ov.at[u], vol_out.at[u], osem.at[0, u]),
            pltpu.make_async_copy(ol.at[u], lft_out.at[u], osem.at[1, u]),
        )

    def step(n, _):
        u = lax.rem(n + 1, 8)
        mark2 = jnp.concatenate(
            [jnp.full((8, 128), 2.0 * marks[u, k].astype(F32), F32) for k in range(6)], axis=0
        )

        def edge(side, f):
            return jnp.sum(jnp.where(lane == u + 8 * f, cin[side], 0.0), axis=1, keepdims=True)

        here = surface(u, 0)
        v_left = jnp.where(g > 0, relax_v(edge(0, 0), here), 0.0)
        l_left = jnp.where(g > 0, relax_l(edge(0, 1), here), 0.0)
        here = surface(u, 9)
        v_right = jnp.where(g < 3, relax_v(edge(1, 0), here), 0.0)
        l_right = jnp.where(g < 3, relax_l(edge(1, 1), here), 0.0)
        v = rv[u, :, group(0)]
        l = rl[u + 1, :, group(0)]
        v_fore, l_fore = pltpu.roll(v_left, 1, 1), pltpu.roll(l_left, 1, 1)
        v_back, l_back = pltpu.roll(v, 127, 1), pltpu.roll(l, 127, 1)
        for i in range(8):
            if i < 7:
                v_then, l_then = rv[u, :, group(i + 1)], rl[u + 1, :, group(i + 1)]
            else:
                v_then, l_then = v_right, l_right
            v_fore_own, l_fore_own = pltpu.roll(v, 1, 1), pltpu.roll(l, 1, 1)
            v_back_then, l_back_then = pltpu.roll(v_then, 127, 1), pltpu.roll(l_then, 127, 1)
            v_y = jnp.where(lane == 0, v_fore, v_fore_own) + jnp.where(lane == 127, v_back_then, v_back)
            l_y = jnp.where(lane == 0, l_fore, l_fore_own) + jnp.where(lane == 127, l_back_then, l_back)
            face = jnp.maximum(l, 0.0) * v + jnp.minimum(l, 0.0) * pltpu.roll(v, 47, 0)
            face = jnp.where(row == 47, 0.0, face)
            div = face - pltpu.roll(face, 1, 0)
            upwind = flux[u + 1, :, group(i)] - flux[u, :, group(i)]
            sharpen = mark2 * (v * (1.0 - v) * (2.0 * v - 1.0))
            ov[u, :, group(i)] = v - 0.3 * (upwind + div) + 0.1 * (v_y - 2.0 * v) + sharpen
            l_z = jnp.where(row == 47, 0.0, pltpu.roll(l, 47, 0)) + jnp.where(row == 0, 0.0, pltpu.roll(l, 1, 0))
            l_x = rl[u + 2, :, group(i)] + rl[u, :, group(i)]
            ol[u, :, group(i)] = l + 0.15 * (l_x + l_y + l_z - 6.0 * l)
            v, l = v_then, l_then
            v_fore, l_fore, v_back, l_back = v_fore_own, l_fore_own, v_back_then, l_back_then
        for c in put_out(u):
            c.start()
        return 0

    lax.fori_loop(0, 6, step, 0)
    for c in rows + onward + [backward]:
        c.wait_recv()
    for i in range(8):
        here = surface(8, i + 1)
        v = relax_v(planes[0, :, group(i)], here)
        l = relax_l(planes[2, :, group(i)], here)
        flux[0, :, group(i)] = jnp.where(s > 0, planes[1, :, group(i)] * v, 0.0)
        rl[0, :, group(i)] = jnp.where(s > 0, l, 0.0)
        l = relax_l(planes[3, :, group(i)], surface(9, i + 1))
        rl[9, :, group(i)] = jnp.where(s < 63, l, 0.0)
    lax.fori_loop(6, 8, step, 0)

    for c in sent:
        c.wait_send()

    @pl.when(high_edge)
    def _():
        for c in up + onward_far + [across]:
            c.wait_send()

    @pl.when(jnp.logical_not(high_edge))
    def _():
        for c in onward:
            c.wait_send()

    @pl.when(low_edge)
    def _():
        down.wait_send()
        upward.wait_send()
        backward_far.wait_send()

    @pl.when(jnp.logical_not(low_edge))
    def _():
        backward.wait_send()

    for u in range(8):
        for c in put_out(u):
            c.wait()


def pass_on(a, b, a_out, b_out, held, sem, sem_out):
    pairs = [(k, i) for i in range(8) for k in range(2)]
    loads = [pltpu.make_async_copy((a, b)[k].at[i], held.at[k, i], sem.at[k, i]) for k, i in pairs]
    stores = [pltpu.make_async_copy(held.at[k, i], (a_out, b_out)[k].at[i], sem_out.at[k, i]) for k, i in pairs]
    for c in loads:
        c.start()
    for load, store in zip(loads, stores):
        load.wait()
        store.start()
    for c in stores:
        c.wait()


def on_device(eta_hat, phi_hat, zone_rows, zone_count, volume, lift, stream_speed, surface_blocks):
    smem = pl.BlockSpec(memory_space=pltpu.SMEM)
    anyw = pl.BlockSpec(memory_space=pl.ANY)
    field = jax.ShapeDtypeStruct((8, 48, 1024), F32)
    results = pl.pallas_call(
        wave_kernel,
        out_shape=(field, field),
        in_specs=[anyw, smem, smem, anyw, anyw, anyw, anyw, anyw],
        out_specs=(anyw, anyw),
        scratch_shapes=[
            pltpu.VMEM((10, 4, EXT), F32),
            pltpu.VMEM((4, 48, 1024), F32),
            pltpu.VMEM((2, 48, 128), F32),
            pltpu.VMEM((2, 48, 128), F32),
            pltpu.VMEM((2, 2, 8, 48, 128), F32),
            pltpu.VMEM((8, 48, 1024), F32),
            pltpu.VMEM((8, 48, 1024), F32),
            pltpu.VMEM((8, 48, 1024), F32),
            pltpu.VMEM((8, 48, 1024), F32),
            pltpu.VMEM((10, 48, 1024), F32),
            pltpu.VMEM((9, 48, 1024), F32),
            pltpu.VMEM((8, 48, 1024), F32),
            pltpu.VMEM((8, 48, 1024), F32),
            pltpu.VMEM((2, 2, 4, 64, 512), F32),
            pltpu.VMEM((2, 4, 4, 2, 8, 256), F32),
            pltpu.VMEM((2, 4, 4, 3, 8, 512), F32),
            pltpu.VMEM((2, 2, 2, 3, 8, 512), F32),
            pltpu.VMEM((2, 2, 4, 3, 8, 512), F32),
            pltpu.VMEM((2, 4, 3, 8, 512), F32),
            pltpu.VMEM((2, 3, 8, 512), F32),
            pltpu.VMEM((2, 2, 3, 8, 512), F32),
            pltpu.VMEM((4, 3, 8, 1024), F32),
            pltpu.VMEM((3, 8, 1024), F32),
            pltpu.VMEM((512, 1024), BF16),
            pltpu.VMEM((512, 1024), BF16),
            pltpu.VMEM((1024, 1024), BF16),
            pltpu.VMEM((8, 32, 512), F32),
            pltpu.VMEM((8, 32, 1024), F32),
            pltpu.VMEM((4, 8, EXT), F32),
            pltpu.VMEM((3, 48, 1024), F32),
            pltpu.VMEM((8, 64), jnp.int32),
            pltpu.VMEM((64, 1024), F32),
            pltpu.SemaphoreType.DMA((N_SEM,)),
            pltpu.SemaphoreType.DMA((N_SEM,)),
            pltpu.SemaphoreType.DMA((11,)),
            pltpu.SemaphoreType.DMA((2, 8)),
        ],
        compiler_params=pltpu.CompilerParams(
            collective_id=0, has_side_effects=True, vmem_limit_bytes=60 * 1024 * 1024
        ),
        name="wave_part",
    )(zone_rows.T, zone_count, surface_blocks, eta_hat, phi_hat, volume, lift, stream_speed)
    return pl.pallas_call(
        pass_on,
        out_shape=(field, field),
        in_specs=[anyw, anyw],
        out_specs=(anyw, anyw),
        scratch_shapes=[pltpu.VMEM((2, 8, 48, 1024), F32), pltpu.SemaphoreType.DMA((2, 8)), pltpu.SemaphoreType.DMA((2, 8))],
        compiler_params=pltpu.CompilerParams(vmem_limit_bytes=60 * 1024 * 1024),
        name="pass_on",
    )(*results)


def solution(mesh):
    return jax.shard_map(
        on_device,
        mesh=mesh,
        in_specs=(
            P("stream", "girth"),
            P("stream", "girth"),
            P(),
            P("stream"),
            P("stream", None, "girth"),
            P("stream", None, "girth"),
            P("stream", None, "girth"),
            P("stream", None),
        ),
        out_specs=(P("stream", None, "girth"), P("stream", None, "girth")),
        check_vma=False,
    )
```

```python
import math

import jax
import jax.numpy as jnp
from jax import lax
from jax.experimental import pallas as pl
from jax.experimental.pallas import tpu as pltpu
from jax.sharding import PartitionSpec as P

F32 = jnp.float32
BF16 = jnp.bfloat16
MESH = pl.DeviceIdType.MESH
EXT = 1280

AG, RS, RZ, GA, ROWS, COLS, PLANES, RELAY = 0, 12, 24, 30, 33, 35, 37, 42
N_SEM = 47


def iota(shape, dim):
    return lax.broadcasted_iota(jnp.int32, shape, dim)


def quarter_turns(t):
    k = jnp.floor(t + 0.5)
    r = t - k
    r2 = r * r
    s = r * (
        1.5707963267949
        + r2 * (-0.645964097506 + r2 * (0.0796926262462 + r2 * (-0.00468175413532 + r2 * 0.000160441184787)))
    )
    c = 1.0 + r2 * (
        -1.23370055013617
        + r2 * (0.253669507901 + r2 * (-0.0208634807634 + r2 * (0.000919260274839 - r2 * 2.52020423731e-5)))
    )
    half = jnp.floor(k * 0.5)
    odd = (k - 2.0 * half) > 0.5
    sign = 1.0 - 2.0 * (half - 2.0 * jnp.floor(half * 0.5))
    return sign, odd, c, s


def cas_dcas(t):
    sign, odd, c, s = quarter_turns(t)
    plus, minus = c + s, c - s
    return sign * jnp.where(odd, minus, plus), sign * jnp.where(odd, -plus, minus)


def cos_sin(t):
    sign, odd, c, s = quarter_turns(t)
    return sign * jnp.where(odd, -s, c), sign * jnp.where(odd, c, s)


def split(value):
    hi = value.astype(BF16)
    return hi, (value - hi.astype(F32)).astype(BF16)


def dot(left, right):
    return jnp.dot(left, right, preferred_element_type=F32)


def dot3(left, right):
    (lh, ll), (rh, rl) = left, right
    return dot(jnp.concatenate([lh, ll, lh], axis=1), jnp.concatenate([rh, rh, rl], axis=0))


def pick(index, values):
    out = values[-1]
    for i in range(len(values) - 2, -1, -1):
        out = jnp.where(index == i, values[i], out)
    return out


def wave_kernel(
    zr_hbm, zc_ref, marks, eta, phi_hbm, vol, lft, spd,
    vol_out, lft_out,
    hr, planes, cin, cmsg, ecol, vv, lv, sv, rv, rl, flux, ov, ol,
    ag, tab, ps, ob, nb, zs, zo, zn, xg, xp, e_hi, e_lo, perm, lhs, uu, hh, relay, zr_ref, phi,
    ssem, rsem, lsem, osem,
):
    s = lax.axis_index("stream")
    g = lax.axis_index("girth")
    zh, y, x = s // 16, (s // 4) % 4, s % 4

    def at(zh_, y_, x_):
        return (zh_ * 16 + y_ * 4 + x_, g)

    def turn(c, d):
        return lax.rem(c + d + 4, 4)

    def on_x(d):
        return at(zh, y, turn(x, d))

    def on_y(d):
        return at(zh, turn(y, d), x)

    def on_z(d):
        return at(turn(zh, d), y, x)

    fetched = [
        pltpu.make_async_copy(eta.at[:, pl.ds(0, 512)], ag.at[0, 0, 0], lsem.at[0]),
        pltpu.make_async_copy(eta.at[:, pl.ds(512, 512)], ag.at[1, 0, 0], lsem.at[1]),
        pltpu.make_async_copy(phi_hbm, phi, lsem.at[2]),
        pltpu.make_async_copy(zr_hbm, zr_ref, lsem.at[3]),
    ]
    edge_left, edge_right = pl.ds(0, 128), pl.ds(896, 128)
    fields = [
        pltpu.make_async_copy(vol.at[:, :, edge_right], ecol.at[0, 0], lsem.at[4]),
        pltpu.make_async_copy(lft.at[:, :, edge_right], ecol.at[0, 1], lsem.at[5]),
        pltpu.make_async_copy(vol.at[:, :, edge_left], ecol.at[1, 0], lsem.at[6]),
        pltpu.make_async_copy(lft.at[:, :, edge_left], ecol.at[1, 1], lsem.at[7]),
        pltpu.make_async_copy(vol, vv, lsem.at[8]),
        pltpu.make_async_copy(lft, lv, lsem.at[9]),
        pltpu.make_async_copy(spd, sv, lsem.at[10]),
    ]
    for c in fetched:
        c.start()

    s_next = lax.rem(s + 1, 64)
    s_prev = lax.rem(s + 63, 64)

    def girth(j):
        return lax.rem(g + j, 4)

    targets = [on_x(1), on_x(-1), on_y(1), on_y(-1), on_z(1), on_z(-1)]
    targets += [(s, girth(j)) for j in (1, 2, 3)]
    targets += [(s_next, g), (s_prev, g), at(zh, 3 - y, 3 - x)]
    barrier = pltpu.get_barrier_semaphore()
    for device in targets:
        pl.semaphore_signal(barrier, inc=1, device_id=device, device_id_type=MESH)
    pl.semaphore_wait(barrier, len(targets))

    def copy(src, dst, index, device):
        return pltpu.make_async_remote_copy(
            src_ref=src, dst_ref=dst, send_sem=ssem.at[index], recv_sem=rsem.at[index],
            device_id=device, device_id_type=MESH,
        )

    sent = []

    def start(src, dst, index, device):
        c = copy(src, dst, index, device)
        c.start()
        sent.append(c)
        return c

    first = (on_x, on_y)
    second = (on_y, on_x)

    gat = {}
    for q in range(2):
        fetched[q].wait()
        gat[q, 0] = start(ag.at[q, 0, 0], ag.at[q, 0, 1], AG + 6 * q, first[q](1))
        gat[q, 1] = start(ag.at[q, 0, 0], ag.at[q, 0, 2], AG + 6 * q + 1, first[q](-1))
    high_edge = jnp.logical_and(x == 3, y == 3)
    low_edge = jnp.logical_and(x == 0, y == 0)
    high_out, high_in = jnp.logical_and(high_edge, zh < 3), jnp.logical_and(high_edge, zh > 0)
    low_out, low_in = jnp.logical_and(low_edge, zh > 0), jnp.logical_and(low_edge, zh < 3)

    def piece(ref, k):
        return ref.at[k] if k < 2 else ref.at[2, pl.ds(0, 24) if k == 3 else pl.ds(24, 24)]

    def own(k):
        return (vol.at[7], spd.at[7], lft.at[7, pl.ds(24, 24)], lft.at[7, pl.ds(0, 24)])[k]

    up = [copy(own(k), piece(relay, k), RELAY + k, on_z(1)) for k in (0, 1, 3)]
    across = copy(own(2), piece(relay, 2), RELAY + 2, at(zh, 0, 0))
    upward = copy(piece(relay, 2), piece(planes, 2), PLANES + 2, on_z(1))
    down = copy(lft.at[0], relay.at[0], RELAY + 4, on_z(-1))

    @pl.when(high_out)
    def _():
        for c in up:
            c.start()

    @pl.when(low_out)
    def _():
        down.start()

    fetched[2].wait()
    kx_own = (s * 64 + iota((64, 1), 0)).astype(F32)
    fx_own = kx_own / 2048.0 - jnp.where(kx_own >= 2048.0, 2.0, 0.0)
    for q in range(2):
        cs = pl.ds(q * 512, 512)
        ky = (g * 1024 + q * 512 + iota((1, 512), 1)).astype(F32)
        fy = ky / 2048.0 - jnp.where(ky >= 2048.0, 2.0, 0.0)
        rad = jnp.sqrt(fx_own * fx_own + fy * fy)
        ag[q, 1, 0] = rad * jnp.tanh(2.0 * rad) * phi[:, cs]
        gat[q, 2] = start(ag.at[q, 1, 0], ag.at[q, 1, 1], AG + 6 * q + 2, first[q](1))
        gat[q, 3] = start(ag.at[q, 1, 0], ag.at[q, 1, 2], AG + 6 * q + 3, first[q](-1))

    fetched[3].wait()
    zr = zr_ref[...].astype(F32)
    lane64 = iota((8, 64), 1)
    lane256 = iota((1, 256), 1)
    slot = lane256 // 64
    rel = (0, 1, -1, 2)
    for q in range(2):
        here = x if q == 0 else y
        coords = [turn(here, d) for d in (0, -1, 1, 2)]
        if q == 0:
            slabs = [zh * 16 + y * 4 + c for c in coords]
        else:
            slabs = [zh * 16 + c * 4 + x for c in coords]
        kx = (pick(slot, slabs) * 64 + lane256 % 64).astype(F32)
        fx = kx / 2048.0 - jnp.where(kx >= 2048.0, 2.0, 0.0)
        for r in range(4):
            for z in range(4):
                zz = turn(zh, rel[z])
                want = zz * 16 + (turn(y, rel[r]) * 4 + x if q == 0 else y * 4 + turn(x, rel[r]))
                rows = jnp.sum(jnp.where(lane64 == want, zr, 0.0), axis=1, keepdims=True)
                t = rows * kx * (1.0 / 1024.0)
                even, odd = cas_dcas(t)
                tab[q, r, z, 0] = even
                tab[q, r, z, 1] = odd * fx

    for q in range(2):
        gat[q, 0].wait_recv()
        gat[q, 4] = start(ag.at[q, 0, 1], ag.at[q, 0, 3], AG + 6 * q + 4, first[q](1))
    for q in range(2):
        gat[q, 3].wait_recv()
        gat[q, 5] = start(ag.at[q, 1, 2], ag.at[q, 1, 3], AG + 6 * q + 5, first[q](-1))

    def fill_e(i, _):
        row = pl.multiple_of(i * 32, 32)
        a = (row + iota((32, 1), 0)).astype(F32)
        c = iota((1, 512), 1).astype(F32)
        co, si = cos_sin(a * c * (1.0 / 128.0))
        for k, value in enumerate((co, si)):
            hi, lo = split(value)
            e_hi[pl.ds(row, 32), k * 512 : (k + 1) * 512] = hi
            e_lo[pl.ds(row, 32), k * 512 : (k + 1) * 512] = lo
        return 0

    lax.fori_loop(0, 16, fill_e, 0)

    def fill_p(i, _):
        row = pl.multiple_of(i * 32, 32)
        a = row + iota((32, 1024), 0)
        b = iota((32, 1024), 1)
        perm[pl.ds(row, 32), :] = jnp.where(a == 8 * (b % 128) + b // 128, 1.0, 0.0).astype(BF16)
        return 0

    lax.fori_loop(0, 32, fill_p, 0)

    near, mid = {}, {}
    for q in range(2):
        for k in (1, 2, 4, 5):
            gat[q, k].wait_recv()
        table = tab[q]
        both = split(table.reshape(256, 256))
        even = split(table[:, :, 0].reshape(128, 256))
        acc = dot3(both, split(ag[q, 0].reshape(256, 512)))
        ps[q, :, :, 0:2] = acc.reshape(4, 4, 2, 8, 512)
        acc = dot3(even, split(ag[q, 1].reshape(256, 512)))
        ps[q, :, :, 2] = acc.reshape(4, 4, 8, 512)
        b = RS + 6 * q
        right, left = second[q](1), second[q](-1)
        near[q, 0] = start(ps.at[q, 3, pl.ds(0, 2)], ob.at[q, 0], b, right)
        near[q, 1] = start(ps.at[q, 3, pl.ds(2, 2)], ob.at[q, 1], b + 1, left)
        near[q, 2] = start(ps.at[q, 1, pl.ds(2, 2)], nb.at[q, 0, pl.ds(2, 2)], b + 2, right)
        near[q, 3] = start(ps.at[q, 2, pl.ds(0, 2)], nb.at[q, 1, pl.ds(0, 2)], b + 3, left)
    for q in range(2):
        b = RS + 6 * q
        right, left = second[q](1), second[q](-1)
        near[q, 0].wait_recv()
        ps[q, 1, 0:2] = ps[q, 1, 0:2] + ob[q, 0]
        near[q, 4] = start(ps.at[q, 1, pl.ds(0, 2)], nb.at[q, 0, pl.ds(0, 2)], b + 4, right)
        near[q, 1].wait_recv()
        ps[q, 2, 2:4] = ps[q, 2, 2:4] + ob[q, 1]
        near[q, 5] = start(ps.at[q, 2, pl.ds(2, 2)], nb.at[q, 1, pl.ds(2, 2)], b + 5, left)

    for c in fields:
        c.start()
    for c in fields[:4]:
        c.wait()
    lane = iota((48, 128), 1)
    for side, at_lane in ((0, 127), (1, 0)):
        packed = jnp.zeros((48, 128), F32)
        for f in range(2):
            for p in range(8):
                packed = jnp.where(lane == 8 * f + p, ecol[side, f, p, :, at_lane : at_lane + 1], packed)
        cmsg[side] = packed
    raw = [
        start(cmsg.at[0], cin.at[0], COLS, (s, girth(1))),
        start(cmsg.at[1], cin.at[1], COLS + 1, (s, girth(3))),
    ]

    onward = [copy(own(k), piece(planes, k), PLANES + k, (s_next, g)) for k in range(4)]
    onward_far = [copy(piece(relay, k), piece(planes, k), PLANES + k, at(zh, 0, 0)) for k in (0, 1, 3)]
    backward = copy(lft.at[0], planes.at[3], PLANES + 4, (s_prev, g))
    backward_far = copy(relay.at[0], planes.at[3], PLANES + 4, at(zh, 3, 3))

    @pl.when(high_out)
    def _():
        across.start()

    @pl.when(jnp.logical_not(high_edge))
    def _():
        for c in onward:
            c.start()

    @pl.when(jnp.logical_not(low_edge))
    def _():
        backward.start()

    right, left = on_z(1), on_z(-1)
    for q in range(2):
        for k in (2, 3, 4, 5):
            near[q, k].wait_recv()
        zs[q] = ps[q, 0] + nb[q, 0] + nb[q, 1]
        b = RZ + 3 * q
        ahead, back = (right, left) if q == 0 else (left, right)
        fore, aft = (1, 2) if q == 0 else (2, 1)
        mid[q, 0] = start(zs.at[q, 3], zo.at[q], b, ahead)
        mid[q, 1] = start(zs.at[q, aft], zn.at[q, 1], b + 1, back)
    for q in range(2):
        b = RZ + 3 * q
        ahead = right if q == 0 else left
        fore = 1 if q == 0 else 2
        mid[q, 0].wait_recv()
        zs[q, fore] = zs[q, fore] + zo[q]
        mid[q, 2] = start(zs.at[q, fore], zn.at[q, 0], b + 2, ahead)
    for q in range(2):
        mid[q, 1].wait_recv()
        mid[q, 2].wait_recv()
        xp[:, :, q * 512 : (q + 1) * 512] = zs[q, 0] + zn[q, 0] + zn[q, 1]

    @pl.when(high_in)
    def _():
        for c, d in zip(up, onward_far):
            c.wait_recv()
            d.start()

    @pl.when(low_in)
    def _():
        down.wait_recv()
        backward_far.start()

    hi, lo = split(xp[...].reshape(24, 1024))
    moved = dot(jnp.concatenate([hi, lo], axis=0), perm[...])
    moved = (moved[:24] + moved[24:]).reshape(3, 8, 1024)
    xg[g] = moved
    beside, over = g + 1 - 2 * lax.rem(g, 2), girth(2)
    far = start(xg.at[g], xg.at[g], GA, (s, over))
    last = [start(xg.at[g], xg.at[g], GA + 1, (s, beside))]
    far.wait_recv()
    last.append(start(xg.at[over], xg.at[over], GA + 2, (s, beside)))
    for c in last:
        c.wait_recv()

    @pl.when(low_in)
    def _():
        across.wait_recv()
        upward.start()

    for gg in range(4):
        os = slice(128 * gg, 128 * (gg + 1))
        for b in range(8):
            ks = slice(128 * b, 128 * (b + 1))
            ky = (1024 * gg + b + 8 * iota((1, 128), 1)).astype(F32)
            fy = ky * (1.0 / 2048.0) - (2.0 if gg >= 2 else 0.0)
            top = xg[gg, 0, :, ks]
            lhs[b, 0:8, os] = top
            lhs[b, 8:16, os] = xg[gg, 1, :, ks]
            lhs[b, 16:24, os] = xg[gg, 2, :, ks]
            lhs[b, 24:32, os] = top * fy
    uu[...] = dot3(split(lhs[...].reshape(256, 512)), (e_hi[...], e_lo[...])).reshape(8, 32, 1024)

    places = [(2 * g - 1, 384)] + [(2 * g + i // 4, 128 * (i % 4)) for i in range(8)] + [(2 * g + 2, 0)]
    b8 = iota((8, 128), 0)
    for i, (block, c0) in enumerate(places):
        c = c0 + iota((8, 128), 1)
        t = (b8 * c).astype(F32) * (1.0 / 1024.0) + (b8 * block).astype(F32) * 0.5
        even, odd = cas_dcas(t)
        out = [jnp.zeros((8, 128), F32) for _ in range(4)]
        for b in range(8):
            ev, od = even[b : b + 1], odd[b : b + 1]
            for k in range(4):
                re = uu[b, 8 * k : 8 * k + 8, c0 : c0 + 128]
                im = uu[b, 8 * k : 8 * k + 8, 512 + c0 : 512 + c0 + 128]
                out[k] = out[k] + (re * ev + im * od if k < 3 else re * od - im * ev)
        cs = slice(128 * i, 128 * (i + 1))
        for k in range(4):
            hh[k, :, cs] = out[k]

    plane = iota((8, 128), 0).astype(F32)
    count = jnp.full((8, 128), zc_ref[0].astype(F32))
    q_ = jnp.minimum((plane + 0.5) / count, 1.0)
    w = 1.0 - (jnp.exp(q_ * q_ * q_ * jnp.sqrt(q_)) - 1.0) / (math.e - 1.0)
    w = jnp.where(plane < count, w, 0.0)
    for i in range(10):
        cs = slice(128 * i, 128 * (i + 1))
        height, tilt_x, lift, tilt_y = (hh[k, :, cs] for k in range(4))
        rise = (1.0 + tilt_x * tilt_x + tilt_y * tilt_y) * lift
        parts = (0.5 + 8.0 * height, jnp.exp(-0.5 * height), w * rise, w)
        for p in range(8):
            for k in range(4):
                hr[p, k : k + 1, cs] = parts[k][p : p + 1]

    row_next = copy(hr.at[7], hr.at[8], ROWS, (s_next, g))
    row_prev = copy(hr.at[0], hr.at[9], ROWS + 1, (s_prev, g))

    @pl.when(s < 63)
    def _():
        row_next.start()

    @pl.when(s > 0)
    def _():
        row_prev.start()


    for c in fields[4:]:
        c.wait()
    level8 = iota((48, 128), 0).astype(F32) - 23.5
    rise_z = jnp.exp(level8 * 0.0625)
    row = iota((48, 128), 0)

    def group(i):
        return slice(128 * i, 128 * (i + 1))

    def surface(plane, i):
        return [hr[plane, k : k + 1, group(i)] for k in range(4)]

    def relax_v(v, here):
        goal = jnp.clip(here[0] - level8, 0.0, 1.0)
        return here[3] * goal + (1.0 - here[3]) * v

    def relax_l(l, here):
        return here[2] * jnp.minimum(rise_z * here[1], 1.0) + (1.0 - here[3]) * l

    def relax_plane(p, _):
        for i in range(8):
            here = surface(p, i + 1)
            v = relax_v(vv[p, :, group(i)], here)
            rv[p, :, group(i)] = v
            flux[p + 1, :, group(i)] = sv[p, :, group(i)] * v
            rl[p + 1, :, group(i)] = relax_l(lv[p, :, group(i)], here)
        return 0

    lax.fori_loop(0, 8, relax_plane, 0)
    for c in raw:
        c.wait_recv()

    def put_out(u):
        return (
            pltpu.make_async_copy(ov.at[u], vol_out.at[u], osem.at[0, u]),
            pltpu.make_async_copy(ol.at[u], lft_out.at[u], osem.at[1, u]),
        )

    def step(n, _):
        u = lax.rem(n + 1, 8)
        mark2 = jnp.concatenate(
            [jnp.full((8, 128), 2.0 * marks[u, k].astype(F32), F32) for k in range(6)], axis=0
        )

        def edge(side, f):
            return jnp.sum(jnp.where(lane == u + 8 * f, cin[side], 0.0), axis=1, keepdims=True)

        here = surface(u, 0)
        v_left = jnp.where(g > 0, relax_v(edge(0, 0), here), 0.0)
        l_left = jnp.where(g > 0, relax_l(edge(0, 1), here), 0.0)
        here = surface(u, 9)
        v_right = jnp.where(g < 3, relax_v(edge(1, 0), here), 0.0)
        l_right = jnp.where(g < 3, relax_l(edge(1, 1), here), 0.0)
        v = rv[u, :, group(0)]
        l = rl[u + 1, :, group(0)]
        v_fore, l_fore = pltpu.roll(v_left, 1, 1), pltpu.roll(l_left, 1, 1)
        v_back, l_back = pltpu.roll(v, 127, 1), pltpu.roll(l, 127, 1)
        for i in range(8):
            if i < 7:
                v_then, l_then = rv[u, :, group(i + 1)], rl[u + 1, :, group(i + 1)]
            else:
                v_then, l_then = v_right, l_right
            v_fore_own, l_fore_own = pltpu.roll(v, 1, 1), pltpu.roll(l, 1, 1)
            v_back_then, l_back_then = pltpu.roll(v_then, 127, 1), pltpu.roll(l_then, 127, 1)
            v_y = jnp.where(lane == 0, v_fore, v_fore_own) + jnp.where(lane == 127, v_back_then, v_back)
            l_y = jnp.where(lane == 0, l_fore, l_fore_own) + jnp.where(lane == 127, l_back_then, l_back)
            face = jnp.maximum(l, 0.0) * v + jnp.minimum(l, 0.0) * pltpu.roll(v, 47, 0)
            face = jnp.where(row == 47, 0.0, face)
            div = face - pltpu.roll(face, 1, 0)
            upwind = flux[u + 1, :, group(i)] - flux[u, :, group(i)]
            sharpen = mark2 * (v * (1.0 - v) * (2.0 * v - 1.0))
            ov[u, :, group(i)] = v - 0.3 * (upwind + div) + 0.1 * (v_y - 2.0 * v) + sharpen
            l_z = jnp.where(row == 47, 0.0, pltpu.roll(l, 47, 0)) + jnp.where(row == 0, 0.0, pltpu.roll(l, 1, 0))
            l_x = rl[u + 2, :, group(i)] + rl[u, :, group(i)]
            ol[u, :, group(i)] = l + 0.15 * (l_x + l_y + l_z - 6.0 * l)
            v, l = v_then, l_then
            v_fore, l_fore, v_back, l_back = v_fore_own, l_fore_own, v_back_then, l_back_then
        for c in put_out(u):
            c.start()
        return 0

    lax.fori_loop(0, 6, step, 0)

    @pl.when(s > 0)
    def _():
        for c in [row_next] + onward:
            c.wait_recv()

    @pl.when(s < 63)
    def _():
        row_prev.wait_recv()
        backward.wait_recv()

    for i in range(8):
        here = surface(8, i + 1)
        v = relax_v(planes[0, :, group(i)], here)
        l = relax_l(planes[2, :, group(i)], here)
        flux[0, :, group(i)] = jnp.where(s > 0, planes[1, :, group(i)] * v, 0.0)
        rl[0, :, group(i)] = jnp.where(s > 0, l, 0.0)
        l = relax_l(planes[3, :, group(i)], surface(9, i + 1))
        rl[9, :, group(i)] = jnp.where(s < 63, l, 0.0)
    lax.fori_loop(6, 8, step, 0)

    for c in sent:
        c.wait_send()

    @pl.when(s < 63)
    def _():
        row_next.wait_send()

    @pl.when(s > 0)
    def _():
        row_prev.wait_send()

    @pl.when(high_out)
    def _():
        for c in up + [across]:
            c.wait_send()

    @pl.when(high_in)
    def _():
        for c in onward_far:
            c.wait_send()

    @pl.when(jnp.logical_not(high_edge))
    def _():
        for c in onward:
            c.wait_send()

    @pl.when(low_out)
    def _():
        down.wait_send()

    @pl.when(low_in)
    def _():
        backward_far.wait_send()
        upward.wait_send()

    @pl.when(jnp.logical_not(low_edge))
    def _():
        backward.wait_send()

    for u in range(8):
        for c in put_out(u):
            c.wait()


def pass_on(a, b, a_out, b_out, held, sem, sem_out):
    pairs = [(k, i) for i in range(8) for k in range(2)]
    loads = [pltpu.make_async_copy((a, b)[k].at[i], held.at[k, i], sem.at[k, i]) for k, i in pairs]
    stores = [pltpu.make_async_copy(held.at[k, i], (a_out, b_out)[k].at[i], sem_out.at[k, i]) for k, i in pairs]
    for c in loads:
        c.start()
    for load, store in zip(loads, stores):
        load.wait()
        store.start()
    for c in stores:
        c.wait()


def on_device(eta_hat, phi_hat, zone_rows, zone_count, volume, lift, stream_speed, surface_blocks):
    smem = pl.BlockSpec(memory_space=pltpu.SMEM)
    anyw = pl.BlockSpec(memory_space=pl.ANY)
    field = jax.ShapeDtypeStruct((8, 48, 1024), F32)
    results = pl.pallas_call(
        wave_kernel,
        out_shape=(field, field),
        in_specs=[anyw, smem, smem, anyw, anyw, anyw, anyw, anyw],
        out_specs=(anyw, anyw),
        scratch_shapes=[
            pltpu.VMEM((10, 4, EXT), F32),
            pltpu.VMEM((4, 48, 1024), F32),
            pltpu.VMEM((2, 48, 128), F32),
            pltpu.VMEM((2, 48, 128), F32),
            pltpu.VMEM((2, 2, 8, 48, 128), F32),
            pltpu.VMEM((8, 48, 1024), F32),
            pltpu.VMEM((8, 48, 1024), F32),
            pltpu.VMEM((8, 48, 1024), F32),
            pltpu.VMEM((8, 48, 1024), F32),
            pltpu.VMEM((10, 48, 1024), F32),
            pltpu.VMEM((9, 48, 1024), F32),
            pltpu.VMEM((8, 48, 1024), F32),
            pltpu.VMEM((8, 48, 1024), F32),
            pltpu.VMEM((2, 2, 4, 64, 512), F32),
            pltpu.VMEM((2, 4, 4, 2, 8, 256), F32),
            pltpu.VMEM((2, 4, 4, 3, 8, 512), F32),
            pltpu.VMEM((2, 2, 2, 3, 8, 512), F32),
            pltpu.VMEM((2, 2, 4, 3, 8, 512), F32),
            pltpu.VMEM((2, 4, 3, 8, 512), F32),
            pltpu.VMEM((2, 3, 8, 512), F32),
            pltpu.VMEM((2, 2, 3, 8, 512), F32),
            pltpu.VMEM((4, 3, 8, 1024), F32),
            pltpu.VMEM((3, 8, 1024), F32),
            pltpu.VMEM((512, 1024), BF16),
            pltpu.VMEM((512, 1024), BF16),
            pltpu.VMEM((1024, 1024), BF16),
            pltpu.VMEM((8, 32, 512), F32),
            pltpu.VMEM((8, 32, 1024), F32),
            pltpu.VMEM((4, 8, EXT), F32),
            pltpu.VMEM((3, 48, 1024), F32),
            pltpu.VMEM((8, 64), jnp.int32),
            pltpu.VMEM((64, 1024), F32),
            pltpu.SemaphoreType.DMA((N_SEM,)),
            pltpu.SemaphoreType.DMA((N_SEM,)),
            pltpu.SemaphoreType.DMA((11,)),
            pltpu.SemaphoreType.DMA((2, 8)),
        ],
        compiler_params=pltpu.CompilerParams(
            collective_id=0, has_side_effects=True, vmem_limit_bytes=60 * 1024 * 1024
        ),
        name="wave_part",
    )(zone_rows.T, zone_count, surface_blocks, eta_hat, phi_hat, volume, lift, stream_speed)
    return pl.pallas_call(
        pass_on,
        out_shape=(field, field),
        in_specs=[anyw, anyw],
        out_specs=(anyw, anyw),
        scratch_shapes=[pltpu.VMEM((2, 8, 48, 1024), F32), pltpu.SemaphoreType.DMA((2, 8)), pltpu.SemaphoreType.DMA((2, 8))],
        compiler_params=pltpu.CompilerParams(vmem_limit_bytes=60 * 1024 * 1024),
        name="pass_on",
    )(*results)


def solution(mesh):
    return jax.shard_map(
        on_device,
        mesh=mesh,
        in_specs=(
            P("stream", "girth"),
            P("stream", "girth"),
            P(),
            P("stream"),
            P("stream", None, "girth"),
            P("stream", None, "girth"),
            P("stream", None, "girth"),
            P("stream", None),
        ),
        out_specs=(P("stream", None, "girth"), P("stream", None, "girth")),
        check_vma=False,
    )
```

```python
import math

import jax
import jax.numpy as jnp
from jax import lax
from jax.experimental import pallas as pl
from jax.experimental.pallas import tpu as pltpu
from jax.sharding import PartitionSpec as P

F32 = jnp.float32
BF16 = jnp.bfloat16
MESH = pl.DeviceIdType.MESH
EXT = 1280

AG, RS, RZ, GA, ROWS, COLS, PLANES, RELAY = 0, 12, 24, 30, 33, 35, 37, 42
N_SEM = 47


def iota(shape, dim):
    return lax.broadcasted_iota(jnp.int32, shape, dim)


def quarter_turns(t):
    k = jnp.floor(t + 0.5)
    r = t - k
    r2 = r * r
    s = r * (
        1.5707963267949
        + r2 * (-0.645964097506 + r2 * (0.0796926262462 + r2 * (-0.00468175413532 + r2 * 0.000160441184787)))
    )
    c = 1.0 + r2 * (
        -1.23370055013617
        + r2 * (0.253669507901 + r2 * (-0.0208634807634 + r2 * (0.000919260274839 - r2 * 2.52020423731e-5)))
    )
    half = jnp.floor(k * 0.5)
    odd = (k - 2.0 * half) > 0.5
    sign = 1.0 - 2.0 * (half - 2.0 * jnp.floor(half * 0.5))
    return sign, odd, c, s


def cas_dcas(t):
    sign, odd, c, s = quarter_turns(t)
    plus, minus = c + s, c - s
    return sign * jnp.where(odd, minus, plus), sign * jnp.where(odd, -plus, minus)


def cos_sin(t):
    sign, odd, c, s = quarter_turns(t)
    return sign * jnp.where(odd, -s, c), sign * jnp.where(odd, c, s)


def split(value):
    hi = value.astype(BF16)
    return hi, (value - hi.astype(F32)).astype(BF16)


def dot(left, right):
    return jnp.dot(left, right, preferred_element_type=F32)


def dot3(left, right):
    (lh, ll), (rh, rl) = left, right
    return dot(jnp.concatenate([lh, ll, lh], axis=1), jnp.concatenate([rh, rh, rl], axis=0))


def pick(index, values):
    out = values[-1]
    for i in range(len(values) - 2, -1, -1):
        out = jnp.where(index == i, values[i], out)
    return out


def wave_kernel(
    zr_hbm, zc_ref, marks, eta, phi_hbm, vol, lft, spd,
    vol_out, lft_out,
    hr, planes, cin, cmsg, ecol, vv, lv, sv, rv, rl, flux, ov, ol,
    ag, tab, ps, ob, nb, zs, zo, zn, xg, xp, e_hi, e_lo, perm, lhs, uu, hh, relay, zr_ref, phi,
    ssem, rsem, lsem, osem,
):
    s = lax.axis_index("stream")
    g = lax.axis_index("girth")
    zh, y, x = s // 16, (s // 4) % 4, s % 4

    def at(zh_, y_, x_):
        return (zh_ * 16 + y_ * 4 + x_, g)

    def turn(c, d):
        return lax.rem(c + d + 4, 4)

    def on_x(d):
        return at(zh, y, turn(x, d))

    def on_y(d):
        return at(zh, turn(y, d), x)

    def on_z(d):
        return at(turn(zh, d), y, x)

    fetched = [
        pltpu.make_async_copy(eta.at[:, pl.ds(0, 512)], ag.at[0, 0, 0], lsem.at[0]),
        pltpu.make_async_copy(eta.at[:, pl.ds(512, 512)], ag.at[1, 0, 0], lsem.at[1]),
        pltpu.make_async_copy(phi_hbm, phi, lsem.at[2]),
        pltpu.make_async_copy(zr_hbm, zr_ref, lsem.at[3]),
    ]
    edge_left, edge_right = pl.ds(0, 128), pl.ds(896, 128)
    fields = [
        pltpu.make_async_copy(vol.at[:, :, edge_right], ecol.at[0, 0], lsem.at[4]),
        pltpu.make_async_copy(lft.at[:, :, edge_right], ecol.at[0, 1], lsem.at[5]),
        pltpu.make_async_copy(vol.at[:, :, edge_left], ecol.at[1, 0], lsem.at[6]),
        pltpu.make_async_copy(lft.at[:, :, edge_left], ecol.at[1, 1], lsem.at[7]),
        pltpu.make_async_copy(vol, vv, lsem.at[8]),
        pltpu.make_async_copy(lft, lv, lsem.at[9]),
        pltpu.make_async_copy(spd, sv, lsem.at[10]),
    ]
    for c in fetched:
        c.start()

    s_next = lax.rem(s + 1, 64)
    s_prev = lax.rem(s + 63, 64)

    def girth(j):
        return lax.rem(g + j, 4)

    targets = [on_x(1), on_x(-1), on_y(1), on_y(-1), on_z(1), on_z(-1)]
    targets += [(s, girth(j)) for j in (1, 2, 3)]
    targets += [(s_next, g), (s_prev, g), at(zh, 3 - y, 3 - x)]
    barrier = pltpu.get_barrier_semaphore()
    for device in targets:
        pl.semaphore_signal(barrier, inc=1, device_id=device, device_id_type=MESH)
    pl.semaphore_wait(barrier, len(targets))

    def copy(src, dst, index, device):
        return pltpu.make_async_remote_copy(
            src_ref=src, dst_ref=dst, send_sem=ssem.at[index], recv_sem=rsem.at[index],
            device_id=device, device_id_type=MESH,
        )

    sent = []

    def start(src, dst, index, device):
        c = copy(src, dst, index, device)
        c.start()
        sent.append(c)
        return c

    first = (on_x, on_y)
    second = (on_y, on_x)

    gat = {}
    for q in range(2):
        fetched[q].wait()
        gat[q, 0] = start(ag.at[q, 0, 0], ag.at[q, 0, 1], AG + 6 * q, first[q](1))
        gat[q, 1] = start(ag.at[q, 0, 0], ag.at[q, 0, 2], AG + 6 * q + 1, first[q](-1))
    high_edge = jnp.logical_and(x == 3, y == 3)
    low_edge = jnp.logical_and(x == 0, y == 0)
    high_out, high_in = jnp.logical_and(high_edge, zh < 3), jnp.logical_and(high_edge, zh > 0)
    low_out, low_in = jnp.logical_and(low_edge, zh > 0), jnp.logical_and(low_edge, zh < 3)

    def piece(ref, k):
        return ref.at[k] if k < 2 else ref.at[2, pl.ds(0, 24) if k == 3 else pl.ds(24, 24)]

    def own(k):
        return (vol.at[7], spd.at[7], lft.at[7, pl.ds(24, 24)], lft.at[7, pl.ds(0, 24)])[k]

    up = [copy(own(k), piece(relay, k), RELAY + k, on_z(1)) for k in (0, 1, 3)]
    across = copy(own(2), piece(relay, 2), RELAY + 2, at(zh, 0, 0))
    upward = copy(piece(relay, 2), piece(planes, 2), PLANES + 2, on_z(1))
    down = copy(lft.at[0], relay.at[0], RELAY + 4, on_z(-1))

    @pl.when(high_out)
    def _():
        for c in up:
            c.start()

    @pl.when(low_out)
    def _():
        down.start()

    fetched[2].wait()
    kx_own = (s * 64 + iota((64, 1), 0)).astype(F32)
    fx_own = kx_own / 2048.0 - jnp.where(kx_own >= 2048.0, 2.0, 0.0)
    for q in range(2):
        cs = pl.ds(q * 512, 512)
        ky = (g * 1024 + q * 512 + iota((1, 512), 1)).astype(F32)
        fy = ky / 2048.0 - jnp.where(ky >= 2048.0, 2.0, 0.0)
        rad = jnp.sqrt(fx_own * fx_own + fy * fy)
        ag[q, 1, 0] = rad * jnp.tanh(2.0 * rad) * phi[:, cs]
        gat[q, 2] = start(ag.at[q, 1, 0], ag.at[q, 1, 1], AG + 6 * q + 2, first[q](1))
        gat[q, 3] = start(ag.at[q, 1, 0], ag.at[q, 1, 2], AG + 6 * q + 3, first[q](-1))

    fetched[3].wait()
    zr = zr_ref[...].astype(F32)
    lane64 = iota((8, 64), 1)
    lane256 = iota((1, 256), 1)
    slot = lane256 // 64
    rel = (0, 1, -1, 2)
    for q in range(2):
        here = x if q == 0 else y
        coords = [turn(here, d) for d in (0, -1, 1, 2)]
        if q == 0:
            slabs = [zh * 16 + y * 4 + c for c in coords]
        else:
            slabs = [zh * 16 + c * 4 + x for c in coords]
        kx = (pick(slot, slabs) * 64 + lane256 % 64).astype(F32)
        fx = kx / 2048.0 - jnp.where(kx >= 2048.0, 2.0, 0.0)
        for r in range(4):
            for z in range(4):
                zz = turn(zh, rel[z])
                want = zz * 16 + (turn(y, rel[r]) * 4 + x if q == 0 else y * 4 + turn(x, rel[r]))
                rows = jnp.sum(jnp.where(lane64 == want, zr, 0.0), axis=1, keepdims=True)
                t = rows * kx * (1.0 / 1024.0)
                even, odd = cas_dcas(t)
                tab[q, r, z, 0] = even
                tab[q, r, z, 1] = odd * fx

    for q in range(2):
        gat[q, 0].wait_recv()
        gat[q, 4] = start(ag.at[q, 0, 1], ag.at[q, 0, 3], AG + 6 * q + 4, first[q](1))
    for q in range(2):
        gat[q, 3].wait_recv()
        gat[q, 5] = start(ag.at[q, 1, 2], ag.at[q, 1, 3], AG + 6 * q + 5, first[q](-1))

    def fill_e(i, _):
        row = pl.multiple_of(i * 32, 32)
        a = (row + iota((32, 1), 0)).astype(F32)
        c = iota((1, 512), 1).astype(F32)
        co, si = cos_sin(a * c * (1.0 / 128.0))
        for k, value in enumerate((co, si)):
            hi, lo = split(value)
            e_hi[pl.ds(row, 32), k * 512 : (k + 1) * 512] = hi
            e_lo[pl.ds(row, 32), k * 512 : (k + 1) * 512] = lo
        return 0

    lax.fori_loop(0, 16, fill_e, 0)

    def fill_p(i, _):
        row = pl.multiple_of(i * 32, 32)
        a = row + iota((32, 1024), 0)
        b = iota((32, 1024), 1)
        perm[pl.ds(row, 32), :] = jnp.where(a == 8 * (b % 128) + b // 128, 1.0, 0.0).astype(BF16)
        return 0

    lax.fori_loop(0, 32, fill_p, 0)

    near, mid = {}, {}
    for q in range(2):
        for k in (1, 2, 4, 5):
            gat[q, k].wait_recv()
        table = tab[q]
        both = split(table.reshape(256, 256))
        even = split(table[:, :, 0].reshape(128, 256))
        acc = dot3(both, split(ag[q, 0].reshape(256, 512)))
        ps[q, :, :, 0:2] = acc.reshape(4, 4, 2, 8, 512)
        acc = dot3(even, split(ag[q, 1].reshape(256, 512)))
        ps[q, :, :, 2] = acc.reshape(4, 4, 8, 512)
        b = RS + 6 * q
        right, left = second[q](1), second[q](-1)
        near[q, 0] = start(ps.at[q, 3, pl.ds(0, 2)], ob.at[q, 0], b, right)
        near[q, 1] = start(ps.at[q, 3, pl.ds(2, 2)], ob.at[q, 1], b + 1, left)
        near[q, 2] = start(ps.at[q, 1, pl.ds(2, 2)], nb.at[q, 0, pl.ds(2, 2)], b + 2, right)
        near[q, 3] = start(ps.at[q, 2, pl.ds(0, 2)], nb.at[q, 1, pl.ds(0, 2)], b + 3, left)
    for q in range(2):
        b = RS + 6 * q
        right, left = second[q](1), second[q](-1)
        near[q, 0].wait_recv()
        ps[q, 1, 0:2] = ps[q, 1, 0:2] + ob[q, 0]
        near[q, 4] = start(ps.at[q, 1, pl.ds(0, 2)], nb.at[q, 0, pl.ds(0, 2)], b + 4, right)
        near[q, 1].wait_recv()
        ps[q, 2, 2:4] = ps[q, 2, 2:4] + ob[q, 1]
        near[q, 5] = start(ps.at[q, 2, pl.ds(2, 2)], nb.at[q, 1, pl.ds(2, 2)], b + 5, left)

    for c in fields:
        c.start()
    for c in fields[:4]:
        c.wait()
    lane = iota((48, 128), 1)
    for side, at_lane in ((0, 127), (1, 0)):
        packed = jnp.zeros((48, 128), F32)
        for f in range(2):
            for p in range(8):
                packed = jnp.where(lane == 8 * f + p, ecol[side, f, p, :, at_lane : at_lane + 1], packed)
        cmsg[side] = packed
    raw = [
        start(cmsg.at[0], cin.at[0], COLS, (s, girth(1))),
        start(cmsg.at[1], cin.at[1], COLS + 1, (s, girth(3))),
    ]

    onward = [copy(own(k), piece(planes, k), PLANES + k, (s_next, g)) for k in range(4)]
    onward_far = [copy(piece(relay, k), piece(planes, k), PLANES + k, at(zh, 0, 0)) for k in (0, 1, 3)]
    backward = copy(lft.at[0], planes.at[3], PLANES + 4, (s_prev, g))
    backward_far = copy(relay.at[0], planes.at[3], PLANES + 4, at(zh, 3, 3))

    @pl.when(high_out)
    def _():
        across.start()

    @pl.when(jnp.logical_not(high_edge))
    def _():
        for c in onward:
            c.start()

    @pl.when(jnp.logical_not(low_edge))
    def _():
        backward.start()

    right, left = on_z(1), on_z(-1)
    for q in range(2):
        for k in (2, 3, 4, 5):
            near[q, k].wait_recv()
        zs[q] = ps[q, 0] + nb[q, 0] + nb[q, 1]
        b = RZ + 3 * q
        ahead, back = (right, left) if q == 0 else (left, right)
        fore, aft = (1, 2) if q == 0 else (2, 1)
        mid[q, 0] = start(zs.at[q, 3], zo.at[q], b, ahead)
        mid[q, 1] = start(zs.at[q, aft], zn.at[q, 1], b + 1, back)
    for q in range(2):
        b = RZ + 3 * q
        ahead = right if q == 0 else left
        fore = 1 if q == 0 else 2
        mid[q, 0].wait_recv()
        zs[q, fore] = zs[q, fore] + zo[q]
        mid[q, 2] = start(zs.at[q, fore], zn.at[q, 0], b + 2, ahead)
    for q in range(2):
        mid[q, 1].wait_recv()
        mid[q, 2].wait_recv()
        xp[:, :, q * 512 : (q + 1) * 512] = zs[q, 0] + zn[q, 0] + zn[q, 1]

    @pl.when(high_in)
    def _():
        for c, d in zip(up, onward_far):
            c.wait_recv()
            d.start()

    @pl.when(low_in)
    def _():
        down.wait_recv()
        backward_far.start()

    hi, lo = split(xp[...].reshape(24, 1024))
    moved = dot(jnp.concatenate([hi, lo], axis=0), perm[...])
    moved = (moved[:24] + moved[24:]).reshape(3, 8, 1024)
    xg[g] = moved
    beside, over = g + 1 - 2 * lax.rem(g, 2), girth(2)
    far = start(xg.at[g], xg.at[g], GA, (s, over))
    last = [start(xg.at[g], xg.at[g], GA + 1, (s, beside))]
    far.wait_recv()
    last.append(start(xg.at[over], xg.at[over], GA + 2, (s, beside)))
    for c in last:
        c.wait_recv()

    @pl.when(low_in)
    def _():
        across.wait_recv()
        upward.start()

    for gg in range(4):
        os = slice(128 * gg, 128 * (gg + 1))
        for b in range(8):
            ks = slice(128 * b, 128 * (b + 1))
            ky = (1024 * gg + b + 8 * iota((1, 128), 1)).astype(F32)
            fy = ky * (1.0 / 2048.0) - (2.0 if gg >= 2 else 0.0)
            top = xg[gg, 0, :, ks]
            lhs[b, 0:8, os] = top
            lhs[b, 8:16, os] = xg[gg, 1, :, ks]
            lhs[b, 16:24, os] = xg[gg, 2, :, ks]
            lhs[b, 24:32, os] = top * fy
    uu[...] = dot3(split(lhs[...].reshape(256, 512)), (e_hi[...], e_lo[...])).reshape(8, 32, 1024)

    places = [(2 * g - 1, 384)] + [(2 * g + i // 4, 128 * (i % 4)) for i in range(8)] + [(2 * g + 2, 0)]
    b8 = iota((8, 128), 0)
    for i, (block, c0) in enumerate(places):
        c = c0 + iota((8, 128), 1)
        t = (b8 * c).astype(F32) * (1.0 / 1024.0) + (b8 * block).astype(F32) * 0.5
        even, odd = cas_dcas(t)
        out = [jnp.zeros((8, 128), F32) for _ in range(4)]
        for b in range(8):
            ev, od = even[b : b + 1], odd[b : b + 1]
            for k in range(4):
                re = uu[b, 8 * k : 8 * k + 8, c0 : c0 + 128]
                im = uu[b, 8 * k : 8 * k + 8, 512 + c0 : 512 + c0 + 128]
                out[k] = out[k] + (re * ev + im * od if k < 3 else re * od - im * ev)
        cs = slice(128 * i, 128 * (i + 1))
        for k in range(4):
            hh[k, :, cs] = out[k]

    plane = iota((8, 128), 0).astype(F32)
    count = jnp.full((8, 128), zc_ref[0].astype(F32))
    q_ = jnp.minimum((plane + 0.5) / count, 1.0)
    w = 1.0 - (jnp.exp(q_ * q_ * q_ * jnp.sqrt(q_)) - 1.0) / (math.e - 1.0)
    w = jnp.where(plane < count, w, 0.0)
    for i in range(10):
        cs = slice(128 * i, 128 * (i + 1))
        height, tilt_x, lift, tilt_y = (hh[k, :, cs] for k in range(4))
        rise = (1.0 + tilt_x * tilt_x + tilt_y * tilt_y) * lift
        parts = (0.5 + 8.0 * height, jnp.exp(-0.5 * height), w * rise, w)
        for p in range(8):
            for k in range(4):
                hr[p, k : k + 1, cs] = parts[k][p : p + 1]

    row_next = copy(hr.at[7], hr.at[8], ROWS, (s_next, g))
    row_prev = copy(hr.at[0], hr.at[9], ROWS + 1, (s_prev, g))

    @pl.when(s < 63)
    def _():
        row_next.start()

    @pl.when(s > 0)
    def _():
        row_prev.start()


    for c in fields[4:]:
        c.wait()
    level8 = iota((48, 128), 0).astype(F32) - 23.5
    rise_z = jnp.exp(level8 * 0.0625)
    row = iota((48, 128), 0)

    def group(i):
        return slice(128 * i, 128 * (i + 1))

    def surface(plane, i):
        return [hr[plane, k : k + 1, group(i)] for k in range(4)]

    def relax_v(v, here):
        goal = jnp.clip(here[0] - level8, 0.0, 1.0)
        return here[3] * goal + (1.0 - here[3]) * v

    def relax_l(l, here):
        return here[2] * jnp.minimum(rise_z * here[1], 1.0) + (1.0 - here[3]) * l

    def relax_plane(p, _):
        for i in range(8):
            here = surface(p, i + 1)
            v = relax_v(vv[p, :, group(i)], here)
            rv[p, :, group(i)] = v
            flux[p + 1, :, group(i)] = sv[p, :, group(i)] * v
            rl[p + 1, :, group(i)] = relax_l(lv[p, :, group(i)], here)
        return 0

    lax.fori_loop(0, 8, relax_plane, 0)
    for c in raw:
        c.wait_recv()

    def put_out(u):
        return (
            pltpu.make_async_copy(ov.at[u], vol_out.at[u], osem.at[0, u]),
            pltpu.make_async_copy(ol.at[u], lft_out.at[u], osem.at[1, u]),
        )

    def step(n, _):
        u = lax.rem(n + 1, 8)
        mark2 = jnp.concatenate(
            [jnp.full((8, 128), 2.0 * marks[u, k].astype(F32), F32) for k in range(6)], axis=0
        )

        def edge(side, f):
            return jnp.sum(jnp.where(lane == u + 8 * f, cin[side], 0.0), axis=1, keepdims=True)

        here = surface(u, 0)
        v_left = jnp.where(g > 0, relax_v(edge(0, 0), here), 0.0)
        l_left = jnp.where(g > 0, relax_l(edge(0, 1), here), 0.0)
        here = surface(u, 9)
        v_right = jnp.where(g < 3, relax_v(edge(1, 0), here), 0.0)
        l_right = jnp.where(g < 3, relax_l(edge(1, 1), here), 0.0)
        v = rv[u, :, group(0)]
        l = rl[u + 1, :, group(0)]
        v_fore, l_fore = pltpu.roll(v_left, 1, 1), pltpu.roll(l_left, 1, 1)
        v_back, l_back = pltpu.roll(v, 127, 1), pltpu.roll(l, 127, 1)
        for i in range(8):
            if i < 7:
                v_then, l_then = rv[u, :, group(i + 1)], rl[u + 1, :, group(i + 1)]
            else:
                v_then, l_then = v_right, l_right
            v_fore_own, l_fore_own = pltpu.roll(v, 1, 1), pltpu.roll(l, 1, 1)
            v_back_then, l_back_then = pltpu.roll(v_then, 127, 1), pltpu.roll(l_then, 127, 1)
            v_y = jnp.where(lane == 0, v_fore, v_fore_own) + jnp.where(lane == 127, v_back_then, v_back)
            l_y = jnp.where(lane == 0, l_fore, l_fore_own) + jnp.where(lane == 127, l_back_then, l_back)
            face = jnp.maximum(l, 0.0) * v + jnp.minimum(l, 0.0) * pltpu.roll(v, 47, 0)
            face = jnp.where(row == 47, 0.0, face)
            div = face - pltpu.roll(face, 1, 0)
            upwind = flux[u + 1, :, group(i)] - flux[u, :, group(i)]
            sharpen = mark2 * (v * (1.0 - v) * (2.0 * v - 1.0))
            ov[u, :, group(i)] = v - 0.3 * (upwind + div) + 0.1 * (v_y - 2.0 * v) + sharpen
            l_z = jnp.where(row == 47, 0.0, pltpu.roll(l, 47, 0)) + jnp.where(row == 0, 0.0, pltpu.roll(l, 1, 0))
            l_x = rl[u + 2, :, group(i)] + rl[u, :, group(i)]
            ol[u, :, group(i)] = l + 0.15 * (l_x + l_y + l_z - 6.0 * l)
            v, l = v_then, l_then
            v_fore, l_fore, v_back, l_back = v_fore_own, l_fore_own, v_back_then, l_back_then
        for c in put_out(u):
            c.start()
        return 0

    lax.fori_loop(0, 6, step, 0)

    @pl.when(s > 0)
    def _():
        for c in [row_next] + onward:
            c.wait_recv()

    @pl.when(s < 63)
    def _():
        row_prev.wait_recv()
        backward.wait_recv()

    for i in range(8):
        here = surface(8, i + 1)
        v = relax_v(planes[0, :, group(i)], here)
        l = relax_l(planes[2, :, group(i)], here)
        flux[0, :, group(i)] = jnp.where(s > 0, planes[1, :, group(i)] * v, 0.0)
        rl[0, :, group(i)] = jnp.where(s > 0, l, 0.0)
        l = relax_l(planes[3, :, group(i)], surface(9, i + 1))
        rl[9, :, group(i)] = jnp.where(s < 63, l, 0.0)
    lax.fori_loop(6, 8, step, 0)

    for c in sent:
        c.wait_send()

    @pl.when(s < 63)
    def _():
        row_next.wait_send()

    @pl.when(s > 0)
    def _():
        row_prev.wait_send()

    @pl.when(high_out)
    def _():
        for c in up + [across]:
            c.wait_send()

    @pl.when(high_in)
    def _():
        for c in onward_far:
            c.wait_send()

    @pl.when(jnp.logical_not(high_edge))
    def _():
        for c in onward:
            c.wait_send()

    @pl.when(low_out)
    def _():
        down.wait_send()

    @pl.when(low_in)
    def _():
        backward_far.wait_send()
        upward.wait_send()

    @pl.when(jnp.logical_not(low_edge))
    def _():
        backward.wait_send()

    for u in range(8):
        for c in put_out(u):
            c.wait()


def pass_on(a, b, a_out, b_out, held, sem, sem_out):
    pairs = [(k, pl.ds(2 * i, 2)) for i in range(4) for k in range(2)]
    loads = [pltpu.make_async_copy((a, b)[k].at[i], held.at[k, i], sem.at[k, n // 2]) for n, (k, i) in enumerate(pairs)]
    stores = [pltpu.make_async_copy(held.at[k, i], (a_out, b_out)[k].at[i], sem_out.at[k, n // 2]) for n, (k, i) in enumerate(pairs)]
    for c in loads:
        c.start()
    for load, store in zip(loads, stores):
        load.wait()
        store.start()
    for c in stores:
        c.wait()


def on_device(eta_hat, phi_hat, zone_rows, zone_count, volume, lift, stream_speed, surface_blocks):
    smem = pl.BlockSpec(memory_space=pltpu.SMEM)
    anyw = pl.BlockSpec(memory_space=pl.ANY)
    field = jax.ShapeDtypeStruct((8, 48, 1024), F32)
    results = pl.pallas_call(
        wave_kernel,
        out_shape=(field, field),
        in_specs=[anyw, smem, smem, anyw, anyw, anyw, anyw, anyw],
        out_specs=(anyw, anyw),
        scratch_shapes=[
            pltpu.VMEM((10, 4, EXT), F32),
            pltpu.VMEM((4, 48, 1024), F32),
            pltpu.VMEM((2, 48, 128), F32),
            pltpu.VMEM((2, 48, 128), F32),
            pltpu.VMEM((2, 2, 8, 48, 128), F32),
            pltpu.VMEM((8, 48, 1024), F32),
            pltpu.VMEM((8, 48, 1024), F32),
            pltpu.VMEM((8, 48, 1024), F32),
            pltpu.VMEM((8, 48, 1024), F32),
            pltpu.VMEM((10, 48, 1024), F32),
            pltpu.VMEM((9, 48, 1024), F32),
            pltpu.VMEM((8, 48, 1024), F32),
            pltpu.VMEM((8, 48, 1024), F32),
            pltpu.VMEM((2, 2, 4, 64, 512), F32),
            pltpu.VMEM((2, 4, 4, 2, 8, 256), F32),
            pltpu.VMEM((2, 4, 4, 3, 8, 512), F32),
            pltpu.VMEM((2, 2, 2, 3, 8, 512), F32),
            pltpu.VMEM((2, 2, 4, 3, 8, 512), F32),
            pltpu.VMEM((2, 4, 3, 8, 512), F32),
            pltpu.VMEM((2, 3, 8, 512), F32),
            pltpu.VMEM((2, 2, 3, 8, 512), F32),
            pltpu.VMEM((4, 3, 8, 1024), F32),
            pltpu.VMEM((3, 8, 1024), F32),
            pltpu.VMEM((512, 1024), BF16),
            pltpu.VMEM((512, 1024), BF16),
            pltpu.VMEM((1024, 1024), BF16),
            pltpu.VMEM((8, 32, 512), F32),
            pltpu.VMEM((8, 32, 1024), F32),
            pltpu.VMEM((4, 8, EXT), F32),
            pltpu.VMEM((3, 48, 1024), F32),
            pltpu.VMEM((8, 64), jnp.int32),
            pltpu.VMEM((64, 1024), F32),
            pltpu.SemaphoreType.DMA((N_SEM,)),
            pltpu.SemaphoreType.DMA((N_SEM,)),
            pltpu.SemaphoreType.DMA((11,)),
            pltpu.SemaphoreType.DMA((2, 8)),
        ],
        compiler_params=pltpu.CompilerParams(
            collective_id=0, has_side_effects=True, vmem_limit_bytes=60 * 1024 * 1024
        ),
        name="wave_part",
    )(zone_rows.T, zone_count, surface_blocks, eta_hat, phi_hat, volume, lift, stream_speed)
    return pl.pallas_call(
        pass_on,
        out_shape=(field, field),
        in_specs=[anyw, anyw],
        out_specs=(anyw, anyw),
        scratch_shapes=[pltpu.VMEM((2, 8, 48, 1024), F32), pltpu.SemaphoreType.DMA((2, 8)), pltpu.SemaphoreType.DMA((2, 8))],
        compiler_params=pltpu.CompilerParams(vmem_limit_bytes=60 * 1024 * 1024),
        name="pass_on",
    )(*results)


def solution(mesh):
    return jax.shard_map(
        on_device,
        mesh=mesh,
        in_specs=(
            P("stream", "girth"),
            P("stream", "girth"),
            P(),
            P("stream"),
            P("stream", None, "girth"),
            P("stream", None, "girth"),
            P("stream", None, "girth"),
            P("stream", None),
        ),
        out_specs=(P("stream", None, "girth"), P("stream", None, "girth")),
        check_vma=False,
    )
```
